128 devices in a mesh: section: 2 (over x_lo), dp: 64 (over z, y, x_hi, core).
Axes of the slice: x: 4 (x_hi: 2, x_lo: 2; x = x_hi * 2 + x_lo), y: 4, z: 4, core: 2. Of those that a mesh axis runs over, the one named last changes fastest.
Arguments:
- inputs: bfloat16 [2, 4, 10240, 4096], P('section', None, 'dp'), may hold values from -40 to 40
- query_grads: bfloat16 [2, 4, 10240, 4096], P('section', None, 'dp'), may hold values from -40 to 40
- plan: int32 [2, 64, 2], P('section'), may hold values from 0 to 3, as said below
Outputs:
- inverses: bfloat16 [2, 64, 128, 128], P('section')
The draws below stay inside these ranges and needn't reach their ends.
Inputs may be any that keep to these rules, and one draw needn't show every extreme that they name: plan[s, f, 0] is the segment that damps and inverts factor f of segment s (it may be s itself); within one segment's 64 factors no segment is named more than 32 times, and in every segment's block some segment is named exactly 32 times. plan[s, f, 1] is the last micro-batch whose statistics enter that factor.
All inputs are finite; a program needn't handle non-finite values.
Results may differ from the reference program's by a relative error of at most 0.001.
Values may be sent and summed in bfloat16 or wider, within the bound.
A program may use at most 128 MiB of HBM per device.

```python
import jax
import jax.numpy as jnp
from jax import lax

HEAD = 128
HEADS = 32
MICRO = 4
MB_TOK = 160
FAC_SECTION = 64
MOST = 32
N_SECTION = 2
N_DP = 64


def shape_features(key, noise_field):
    subkeys = jax.random.split(key, 3)
    columns = HEADS * HEAD
    rows_all = MB_TOK * N_DP
    blended = noise_field + 0.7 * jnp.roll(noise_field, 1, axis=3) + 0.45 * jnp.roll(noise_field, -2, axis=3)
    column_scale = jnp.exp(jax.random.uniform(subkeys[0], (columns,), minval=-0.6, maxval=0.6))
    batch_scale = jnp.exp(jax.random.uniform(subkeys[1], (N_SECTION, MICRO, 1, 1), minval=-0.6, maxval=0.6))
    device = jnp.arange(rows_all, dtype=jnp.int32) // MB_TOK
    block_ids = jnp.arange(columns, dtype=jnp.int32) // HEAD
    offset = jax.random.randint(subkeys[2], (), 0, N_DP)
    paired = (block_ids[None, :] + offset) % N_DP == device[:, None]
    amplitude = jnp.where(paired, 4.0, 1.0)
    values = blended / 1.3 * column_scale * batch_scale * amplitude
    return jnp.clip(values, -40.0, 40.0)


def draw_inputs(key, part):
    key = jax.random.fold_in(key, 3)
    noise_key = jax.random.fold_in(key, 0)
    shape_key = jax.random.fold_in(key, 2)
    array_shape = (N_SECTION, MICRO, MB_TOK * N_DP, HEADS * HEAD)
    noise_field = jax.random.normal(noise_key, array_shape)
    values = shape_features(shape_key, noise_field)
    return values.astype(jnp.bfloat16)


def draw_query_grads(key, part):
    key = jax.random.fold_in(key, 5)
    noise_key = jax.random.fold_in(key, 0)
    shape_key = jax.random.fold_in(key, 2)
    array_shape = (N_SECTION, MICRO, MB_TOK * N_DP, HEADS * HEAD)
    noise_field = jax.random.normal(noise_key, array_shape)
    values = shape_features(shape_key, noise_field)
    return values.astype(jnp.bfloat16)


def draw_plan(key, part):
    key = jax.random.fold_in(key, 7)
    subkeys = jax.random.split(key, 4)
    busiest = jax.random.randint(subkeys[0], (), 0, N_SECTION)
    positions = jnp.arange(FAC_SECTION, dtype=jnp.int32)
    others = jax.random.randint(subkeys[1], (N_SECTION, FAC_SECTION), 1, N_SECTION)
    target = jnp.where(positions[None, :] < MOST, busiest, (busiest + others) % N_SECTION)
    newest = jax.random.randint(subkeys[2], (N_SECTION, FAC_SECTION), 0, MICRO)
    newest = newest.at[:, 0].set(MICRO - 1).at[:, 1].set(0)
    orders = jax.vmap(lambda sub: jax.random.permutation(sub, FAC_SECTION))(jax.random.split(subkeys[3], N_SECTION))
    target = jnp.take_along_axis(target, orders, axis=1)
    newest = jnp.take_along_axis(newest, orders, axis=1)
    return jnp.stack([target, newest], axis=2).astype(jnp.int32)


def setup_inputs(seed: int = 0) -> dict:
    arg_keys = jax.random.split(jax.random.key(seed), 4)
    inputs = draw_inputs(jax.random.fold_in(arg_keys[3], 71), 0)
    query_grads = draw_query_grads(jax.random.fold_in(arg_keys[3], 71), 0)
    plan = draw_plan(jax.random.fold_in(arg_keys[3], 71), 0)
    return {"inputs": inputs, "query_grads": query_grads, "plan": plan}


DAMPING = 0.3

def invert(factors):
    block_size = factors.shape[-1]
    identity = jnp.eye(block_size, dtype=jnp.float32)
    damped = factors + DAMPING * identity
    lower_factor = jnp.linalg.cholesky(damped)
    right_side = jnp.broadcast_to(identity, damped.shape)
    halfway = lax.linalg.triangular_solve(lower_factor, right_side, left_side=True, lower=True)
    inverse = lax.linalg.triangular_solve(lower_factor, halfway, left_side=True, lower=True, transpose_a=True)
    return inverse.astype(jnp.bfloat16)

def segment_factors(segment_inputs, segment_grads, newest):
    rows_all = segment_inputs.shape[1]
    factors = jnp.zeros((2 * HEADS, HEAD, HEAD), jnp.float32)
    for batch_index in range(MICRO):
        included = (newest >= batch_index).astype(jnp.float32)
        weight = included / (rows_all * (newest + 1).astype(jnp.float32))
        in_blocks = segment_inputs[batch_index].astype(jnp.float32).reshape(rows_all, HEADS, HEAD)
        grad_blocks = segment_grads[batch_index].astype(jnp.float32).reshape(rows_all, HEADS, HEAD)
        in_gram = jnp.einsum('thi,thj->hij', in_blocks, in_blocks, precision=lax.Precision.HIGHEST)
        grad_gram = jnp.einsum('thi,thj->hij', grad_blocks, grad_blocks, precision=lax.Precision.HIGHEST)
        gram_blocks = jnp.concatenate((in_gram, grad_gram), axis=0)
        factors = factors + weight[:, None, None] * gram_blocks
    return factors

def reference(inputs, query_grads, plan):

    def one_segment(operands):
        segment_inputs, segment_grads, routing = operands
        return invert(segment_factors(segment_inputs, segment_grads, routing[:, 1]))
    return lax.map(one_segment, (inputs, query_grads, plan))
```

```python
import functools

import jax
import jax.numpy as jnp
from jax import lax
from jax.experimental import pallas as pl
from jax.experimental.pallas import tpu as pltpu
from jax.sharding import PartitionSpec as P

HEAD = 128
DAMPING = 0.3
MICRO = 4
PAIRS = 16
PACK = 136
CUT = 64
MESH = pl.DeviceIdType.MESH

ORDER = (
    (2, 2), (2, 1), (1, 2), (2, 3),
    (3, 2), (1, 1), (1, 3), (3, 1),
    (3, 3), (2, 0), (0, 2), (1, 0),
    (0, 1), (3, 0), (0, 3), (0, 0),
)
SLOT = {offset: slot for slot, offset in enumerate(ORDER)}
GROUP = 4


def split3(x):
    high = x.astype(jnp.bfloat16)
    x = x - high.astype(jnp.float32)
    middle = x.astype(jnp.bfloat16)
    x = x - middle.astype(jnp.float32)
    return high, middle, x.astype(jnp.bfloat16)


def product(a, b):
    ah, am, al = split3(a)
    bh, bm, bl = split3(b)
    left = jnp.concatenate([ah, ah, am, ah, al, am], 0)
    right = jnp.concatenate([bh, bm, bh, bl, bh, bm], 0)
    return lax.dot_general(left, right, (((0,), (0,)), ((), ())), preferred_element_type=jnp.float32)


def spread(x):
    return jnp.broadcast_to(x, (8, HEAD))


def invert(matrix):
    lane = lax.broadcasted_iota(jnp.int32, (8, HEAD), 1)
    sub = lax.broadcasted_iota(jnp.int32, (8, HEAD), 0)
    rows = [matrix[8 * g : 8 * g + 8, :] for g in range(16)]
    for g in range(16):
        base = 8 * g
        panel = rows[g]
        inside = (lane >= base) & (lane < base + 8)
        columns = [spread(panel[:, base + j : base + j + 1]) for j in range(8)]
        a = {(i, j): spread(columns[j][i : i + 1, :]) for i in range(8) for j in range(i, 8)}
        start = jnp.where(inside, jnp.where(lane - base == sub, 1.0, 0.0), panel)
        w = [spread(start[j : j + 1, :]) for j in range(8)]
        more = g + 1 < 16
        if more:
            following = rows[g + 1]
            c = [spread(following[:, base + j : base + j + 1]) for j in range(8)]
        low = {}
        inverse_d = [None] * 8
        for i in (0, 2, 4, 6):
            p, q, r = a[i, i], a[i, i + 1], a[i + 1, i + 1]
            d0 = 1.0 / p
            d1 = p * (1.0 / (p * r - q * q))
            l10 = q * d0
            inverse_d[i], inverse_d[i + 1] = d0, d1
            low[i + 1, i] = l10
            e0 = {j: a[i, j] for j in range(i + 2, 8)}
            e1 = {j: a[i + 1, j] - l10 * a[i, j] for j in range(i + 2, 8)}
            for j in range(i + 2, 8):
                low[j, i], low[j, i + 1] = e0[j] * d0, e1[j] * d1
            for j in range(i + 2, 8):
                for m in range(j, 8):
                    a[j, m] = a[j, m] - (low[j, i] * e0[m] + low[j, i + 1] * e1[m])
            w[i + 1] = w[i + 1] - l10 * w[i]
            for j in range(i + 2, 8):
                w[j] = w[j] - (low[j, i] * w[i] + low[j, i + 1] * w[i + 1])
            if more:
                c[i + 1] = c[i + 1] - l10 * c[i]
                for j in range(i + 2, 8):
                    c[j] = c[j] - (low[j, i] * c[i] + low[j, i + 1] * c[i + 1])
        z = [inverse_d[j] * w[j] for j in range(8)]
        if more:
            t = [c[j] * z[j] for j in range(8)]
            t = ((t[0] + t[1]) + (t[2] + t[3])) + ((t[4] + t[5]) + (t[6] + t[7]))
            ahead = jnp.where(inside, 0.0, following) - t
        solved = list(z)
        for j in range(7, -1, -1):
            for i in range(j):
                solved[i] = solved[i] - low[j, i] * solved[j]

        def together(parts):
            whole = parts[7]
            for i in range(7):
                whole = jnp.where(sub == i, parts[i], whole)
            return whole

        w_rows, z_rows, solved_rows = together(w), together(z), together(solved)
        left = jnp.where(inside, 0.0, jnp.where(lane < base, -w_rows, w_rows))
        update = product(left, z_rows)
        rows = [
            solved_rows if h == g else jnp.where(inside, 0.0, rows[h]) - update[8 * h : 8 * h + 8, :]
            for h in range(16)
        ]
        if more:
            rows[g + 1] = ahead
    return jnp.concatenate(rows, 0)


def kernel(
    tokens_all,
    inputs_ref, grads_ref, plan_ref, out_ref,
    data, given, taken, sums, in_y, in_z, next_z, next_y, last_in, part_z, part_y, last, result,
    load_sem, core_send, core_recv, y_send, y_recv, z_send, z_recv,
    z2_send, z2_recv, y2_send, y2_recv, x_send, x_recv,
    a1_send, a1_recv, b1_send, b1_recv, a2_send, a2_recv, b2_send, b2_recv,
    c_send, c_recv, out_sem,
):
    section = lax.axis_index("section")
    dp = lax.axis_index("dp")
    z, y, x, core = dp // 16, (dp // 4) % 4, (dp // 2) % 2, dp % 2

    def device(dz=0, dy=0, dx=0, dc=0):
        there = (((z + dz) % 4) * 4 + (y + dy) % 4) * 4 + ((x + dx) % 2) * 2 + (core + dc) % 2
        return (section, there)

    def pair_of(dy, dz):
        return ((y + dy) % 4) * 4 + (z + dz) % 4

    def load(ref, half, slot):
        pair = pair_of(*ORDER[slot])
        return pltpu.make_async_copy(
            ref.at[0, :, :, pl.ds(pl.multiple_of(pair * 256, 256), 256)],
            data.at[half, slot],
            load_sem.at[half, slot],
        )

    for mine, refs in ((0, (grads_ref, inputs_ref)), (1, (inputs_ref, grads_ref))):

        @pl.when(core == mine)
        def _():
            for half in range(2):
                for slot in range(PAIRS):
                    load(refs[half], half, slot).start()

    partners = [device(dc=1)]
    partners += [device(dy=d) for d in (1, 2, 3)] + [device(dz=d) for d in (1, 2, 3)]
    partners += [device(dx=1, dy=d) for d in range(4)] + [device(dx=1, dz=d) for d in (1, 2, 3)]
    barrier = pltpu.get_barrier_semaphore()
    for partner in partners:
        pl.semaphore_signal(barrier, inc=1, device_id=partner, device_id_type=MESH)

    row = lax.broadcasted_iota(jnp.int32, (HEAD, HEAD), 0)
    col = lax.broadcasted_iota(jnp.int32, (HEAD, HEAD), 1)

    def gram(half, slot):
        pair = pair_of(*ORDER[slot])
        whose = core if half else 1 - core
        factor = whose * 32 + pair * 2
        whole = data[half, slot].reshape(-1, 256)
        blocks = []
        for b in range(2):
            newest = plan_ref[0, factor + b, 1]
            own = slice(b * HEAD, (b + 1) * HEAD)
            right = [data[half, slot, 0, :, own]]
            for m in range(1, MICRO):
                kept = jnp.minimum(jnp.maximum(newest - (m - 1), 0), 1).astype(jnp.float32)
                kept = jnp.full((1, HEAD), kept, jnp.float32).astype(jnp.bfloat16)
                right.append(data[half, slot, m, :, own] * kept)
            blocks.append(
                lax.dot_general(
                    whole[:, own],
                    jnp.concatenate(right, 0),
                    (((0,), (0,)), ((), ())),
                    preferred_element_type=jnp.float32,
                )
            )
        packed = jnp.where(row >= col, blocks[0], blocks[1])
        diagonal = jnp.where(row == col, blocks[1], 0.0)
        return packed, jnp.sum(diagonal.reshape(16, 8, HEAD), axis=0)

    def remote(src, dst, send, recv, to):
        return pltpu.make_async_remote_copy(
            src_ref=src, dst_ref=dst, send_sem=send, recv_sem=recv, device_id=to, device_id_type=MESH
        )

    sent = []

    def start(copy):
        copy.start()
        sent.append(copy)

    def core_copy(slot):
        return remote(given.at[slot], taken.at[slot], core_send.at[slot], core_recv.at[slot], device(dc=1))

    for first in range(0, PAIRS, GROUP):
        for slot in range(first, first + GROUP):
            load(inputs_ref, 0, slot).wait()
        for slot in range(first, first + GROUP):
            packed, diagonal = gram(0, slot)
            given[slot, 0:HEAD, :] = packed
            given[slot, HEAD:PACK, :] = diagonal
        if first == 0:
            pl.semaphore_wait(barrier, len(partners))
        for slot in range(first, first + GROUP):
            start(core_copy(slot))

    def y_copy(dy, dz):
        slot = SLOT[dy, dz]
        i = (dy - 1) * 4 + dz
        return remote(sums.at[slot, 0:CUT], in_y.at[i], y_send.at[i], y_recv.at[i], device(dy=dy))

    def z_copy(dy, dz):
        slot = SLOT[dy, dz]
        i = (dz - 1) * 4 + dy
        return remote(sums.at[slot, CUT:PACK], in_z.at[i], z_send.at[i], z_recv.at[i], device(dz=dz))

    for first in range(0, PAIRS, GROUP):
        for slot in range(first, first + GROUP):
            load(inputs_ref, 1, slot).wait()
            core_copy(slot).wait_recv()
        for slot in range(first, first + GROUP):
            packed, diagonal = gram(1, slot)
            sums[slot, 0:HEAD, :] = packed + taken[slot, 0:HEAD, :]
            sums[slot, HEAD:PACK, :] = diagonal + taken[slot, HEAD:PACK, :]
        for slot in range(first, first + GROUP):
            dy, dz = ORDER[slot]
            if dy:
                start(y_copy(dy, dz))
            if dz:
                start(z_copy(dy, dz))

    def z2_copy(dz):
        return remote(part_z.at[dz], next_z.at[dz - 1], z2_send.at[dz - 1], z2_recv.at[dz - 1], device(dz=dz))

    def y2_copy(dy):
        return remote(part_y.at[dy], next_y.at[dy - 1], y2_send.at[dy - 1], y2_recv.at[dy - 1], device(dy=dy))

    for d in (2, 1, 3, 0):
        for o in (1, 2, 3):
            y_copy(o, d).wait_recv()
        part_z[d] = (sums[SLOT[0, d], 0:CUT] + in_y[d]) + (in_y[4 + d] + in_y[8 + d])
        if d:
            start(z2_copy(d))
        for o in (1, 2, 3):
            z_copy(d, o).wait_recv()
        part_y[d] = (sums[SLOT[d, 0], CUT:PACK] + in_z[d]) + (in_z[4 + d] + in_z[8 + d])
        if d:
            start(y2_copy(d))

    for d in (1, 3, 2):
        z2_copy(d).wait_recv()
        y2_copy(d).wait_recv()
    last[0:CUT] = (part_z[0] + next_z[0]) + (next_z[1] + next_z[2])
    last[CUT:PACK] = (part_y[0] + next_y[0]) + (next_y[1] + next_y[2])
    x_copy = remote(last, last_in, x_send.at[0], x_recv.at[0], device(dx=1))
    start(x_copy)
    x_copy.wait_recv()

    packed = last[0:HEAD] + last_in[0:HEAD]
    diagonal = jnp.sum(last[HEAD:PACK] + last_in[HEAD:PACK], axis=0, keepdims=True)
    second = x.astype(jnp.float32)
    triangle = jnp.where((row - col) * (1 - 2 * x) > 0, packed, 0.0)
    diagonal = second * diagonal + (1.0 - second) * packed
    total = triangle + triangle.T + jnp.where(row == col, diagonal, 0.0)
    newest = plan_ref[0, core * 32 + pair_of(0, 0) * 2 + x, 1]
    count = jnp.full((1, HEAD), (newest + 1).astype(jnp.float32), jnp.float32) * float(tokens_all)
    damped = total / count + jnp.where(row == col, DAMPING, 0.0)
    inverse = invert(damped)
    result[core, y, z, x] = inverse.astype(jnp.bfloat16)

    def a1_copy(dx, dy):
        i = dx * 4 + dy - 1
        here = result.at[core, y, z, x, 0:CUT]
        return remote(here, here, a1_send.at[i], a1_recv.at[i], device(dx=dx, dy=dy))

    def b1_copy(dx, dz):
        i = dx * 4 + dz - 1
        here = result.at[core, y, z, x, CUT:HEAD]
        return remote(here, here, b1_send.at[i], b1_recv.at[i], device(dx=dx, dz=dz))

    def a1_arrival(dx, dy):
        i = dx * 4 + dy - 1
        here = result.at[core, (y - dy) % 4, z, (x + dx) % 2, 0:CUT]
        return remote(here, here, a1_send.at[i], a1_recv.at[i], device(dx=dx, dy=dy))

    def b1_arrival(dx, dz):
        i = dx * 4 + dz - 1
        here = result.at[core, y, (z - dz) % 4, (x + dx) % 2, CUT:HEAD]
        return remote(here, here, b1_send.at[i], b1_recv.at[i], device(dx=dx, dz=dz))

    steps = [(0, 2), (0, 1), (0, 3), (1, 0), (1, 2), (1, 1), (1, 3)]
    for dx, d in steps:
        start(a1_copy(dx, d))
        start(b1_copy(dx, d))

    def a2_copy(dy, dz):
        i = dy * 3 + dz - 1
        here = result.at[core, (y - dy) % 4, z, :, 0:CUT]
        return remote(here, here, a2_send.at[i], a2_recv.at[i], device(dz=dz))

    def a2_arrival(dy, dz):
        i = dy * 3 + dz - 1
        here = result.at[core, (y - dy) % 4, (z - dz) % 4, :, 0:CUT]
        return remote(here, here, a2_send.at[i], a2_recv.at[i], device(dz=dz))

    def b2_copy(dz, dy):
        i = dz * 3 + dy - 1
        here = result.at[core, y, (z - dz) % 4, :, CUT:HEAD]
        return remote(here, here, b2_send.at[i], b2_recv.at[i], device(dy=dy))

    def b2_arrival(dz, dy):
        i = dz * 3 + dy - 1
        here = result.at[core, (y - dy) % 4, (z - dz) % 4, :, CUT:HEAD]
        return remote(here, here, b2_send.at[i], b2_recv.at[i], device(dy=dy))

    for d in (0, 1, 3, 2):
        for dx in (0, 1):
            if dx or d:
                a1_arrival(dx, d).wait_recv()
                b1_arrival(dx, d).wait_recv()
        for o in (2, 1, 3):
            start(a2_copy(d, o))
            start(b2_copy(d, o))

    def a3_copy(whose, dz):
        here = result.at[whose, :, (z - dz) % 4, :, 0:CUT]
        return remote(here, here, c_send.at[dz], c_recv.at[dz], device(dc=1))

    def b3_copy(whose, dy):
        here = result.at[whose, (y - dy) % 4, :, :, CUT:HEAD]
        return remote(here, here, c_send.at[4 + dy], c_recv.at[4 + dy], device(dc=1))

    start(a3_copy(core, 0))
    start(b3_copy(core, 0))
    for d in (1, 3, 2):
        for o in range(4):
            a2_arrival(o, d).wait_recv()
        start(a3_copy(core, d))
        for o in range(4):
            b2_arrival(o, d).wait_recv()
        start(b3_copy(core, d))

    def write(whose):
        return pltpu.make_async_copy(result.at[whose], out_ref.at[whose], out_sem.at[whose])

    mine = write(core)
    mine.start()
    for d in range(4):
        a3_copy(1 - core, d).wait_recv()
        b3_copy(1 - core, d).wait_recv()
    theirs = write(1 - core)
    theirs.start()
    for copy in sent:
        copy.wait_send()
    mine.wait()
    theirs.wait()


def shards(inputs, query_grads, plan):
    micro, tokens = inputs.shape[1], inputs.shape[2]
    members = lax.axis_size("dp")
    dma = pltpu.SemaphoreType.DMA
    f32, bf16 = jnp.float32, jnp.bfloat16
    vmem = pltpu.VMEM
    result = pl.pallas_call(
        functools.partial(kernel, tokens * members),
        out_shape=jax.ShapeDtypeStruct((2, 4, 4, 2, HEAD, HEAD), bf16),
        in_specs=[
            pl.BlockSpec(memory_space=pl.ANY),
            pl.BlockSpec(memory_space=pl.ANY),
            pl.BlockSpec(memory_space=pltpu.SMEM),
        ],
        out_specs=pl.BlockSpec(memory_space=pl.ANY),
        scratch_shapes=[
            vmem((2, PAIRS, micro, tokens, 256), bf16),
            vmem((PAIRS, PACK, HEAD), f32),
            vmem((PAIRS, PACK, HEAD), f32),
            vmem((PAIRS, PACK, HEAD), f32),
            vmem((12, CUT, HEAD), f32),
            vmem((12, PACK - CUT, HEAD), f32),
            vmem((3, CUT, HEAD), f32),
            vmem((3, PACK - CUT, HEAD), f32),
            vmem((PACK, HEAD), f32),
            vmem((4, CUT, HEAD), f32),
            vmem((4, PACK - CUT, HEAD), f32),
            vmem((PACK, HEAD), f32),
            vmem((2, 4, 4, 2, HEAD, HEAD), bf16),
            dma((2, PAIRS)),
            dma((PAIRS,)), dma((PAIRS,)),
            dma((12,)), dma((12,)), dma((12,)), dma((12,)),
            dma((3,)), dma((3,)), dma((3,)), dma((3,)),
            dma((1,)), dma((1,)),
            dma((7,)), dma((7,)), dma((7,)), dma((7,)),
            dma((12,)), dma((12,)), dma((12,)), dma((12,)),
            dma((8,)), dma((8,)),
            dma((2,)),
        ],
        compiler_params=pltpu.CompilerParams(
            collective_id=0, has_side_effects=True, vmem_limit_bytes=40 << 20
        ),
        name="factor_inverses",
    )(inputs, query_grads, plan)
    return result.reshape(1, 64, HEAD, HEAD)


def solution(mesh):
    in_specs = (
        P("section", None, "dp", None),
        P("section", None, "dp", None),
        P("section", None, None),
    )
    out_specs = P("section", None, None, None)
    return jax.shard_map(shards, mesh=mesh, in_specs=in_specs, out_specs=out_specs, check_vma=False)
```

```python
import functools

import jax
import jax.numpy as jnp
from jax import lax
from jax.experimental import pallas as pl
from jax.experimental.pallas import tpu as pltpu
from jax.sharding import PartitionSpec as P

HEAD = 128
DAMPING = 0.3
MICRO = 4
PAIRS = 16
PACK = 136
CUT = 64
MESH = pl.DeviceIdType.MESH

ORDER = (
    (2, 2), (2, 1), (1, 2), (2, 3),
    (3, 2), (1, 1), (1, 3), (3, 1),
    (3, 3), (2, 0), (0, 2), (1, 0),
    (0, 1), (3, 0), (0, 3), (0, 0),
)
SLOT = {offset: slot for slot, offset in enumerate(ORDER)}
GROUP = 4
TURNS = ((0, 0), (0, 4), (1, 0), (0, 8), (1, 4), (0, 12), (1, 8), (1, 12))


def split3(x):
    high = x.astype(jnp.bfloat16)
    x = x - high.astype(jnp.float32)
    middle = x.astype(jnp.bfloat16)
    x = x - middle.astype(jnp.float32)
    return high, middle, x.astype(jnp.bfloat16)


def product(a, b):
    ah, am, al = split3(a)
    bh, bm, bl = split3(b)
    left = jnp.concatenate([ah, ah, am, ah, al, am], 0)
    right = jnp.concatenate([bh, bm, bh, bl, bh, bm], 0)
    return lax.dot_general(left, right, (((0,), (0,)), ((), ())), preferred_element_type=jnp.float32)


def spread(x):
    return jnp.broadcast_to(x, (8, HEAD))


def invert(matrix):
    lane = lax.broadcasted_iota(jnp.int32, (8, HEAD), 1)
    sub = lax.broadcasted_iota(jnp.int32, (8, HEAD), 0)
    rows = [matrix[8 * g : 8 * g + 8, :] for g in range(16)]
    for g in range(16):
        base = 8 * g
        panel = rows[g]
        inside = (lane >= base) & (lane < base + 8)
        columns = [spread(panel[:, base + j : base + j + 1]) for j in range(8)]
        a = {(i, j): spread(columns[j][i : i + 1, :]) for i in range(8) for j in range(i, 8)}
        start = jnp.where(inside, jnp.where(lane - base == sub, 1.0, 0.0), panel)
        w = [spread(start[j : j + 1, :]) for j in range(8)]
        more = g + 1 < 16
        if more:
            following = rows[g + 1]
            c = [spread(following[:, base + j : base + j + 1]) for j in range(8)]
        low = {}
        inverse_d = [None] * 8
        for i in (0, 2, 4, 6):
            p, q, r = a[i, i], a[i, i + 1], a[i + 1, i + 1]
            d0 = 1.0 / p
            d1 = p * (1.0 / (p * r - q * q))
            l10 = q * d0
            inverse_d[i], inverse_d[i + 1] = d0, d1
            low[i + 1, i] = l10
            e0 = {j: a[i, j] for j in range(i + 2, 8)}
            e1 = {j: a[i + 1, j] - l10 * a[i, j] for j in range(i + 2, 8)}
            for j in range(i + 2, 8):
                low[j, i], low[j, i + 1] = e0[j] * d0, e1[j] * d1
            for j in range(i + 2, 8):
                for m in range(j, 8):
                    a[j, m] = a[j, m] - (low[j, i] * e0[m] + low[j, i + 1] * e1[m])
            w[i + 1] = w[i + 1] - l10 * w[i]
            for j in range(i + 2, 8):
                w[j] = w[j] - (low[j, i] * w[i] + low[j, i + 1] * w[i + 1])
            if more:
                c[i + 1] = c[i + 1] - l10 * c[i]
                for j in range(i + 2, 8):
                    c[j] = c[j] - (low[j, i] * c[i] + low[j, i + 1] * c[i + 1])
        z = [inverse_d[j] * w[j] for j in range(8)]
        if more:
            t = [c[j] * z[j] for j in range(8)]
            t = ((t[0] + t[1]) + (t[2] + t[3])) + ((t[4] + t[5]) + (t[6] + t[7]))
            ahead = jnp.where(inside, 0.0, following) - t
        solved = list(z)
        for j in range(7, -1, -1):
            for i in range(j):
                solved[i] = solved[i] - low[j, i] * solved[j]

        def together(parts):
            whole = parts[7]
            for i in range(7):
                whole = jnp.where(sub == i, parts[i], whole)
            return whole

        w_rows, z_rows, solved_rows = together(w), together(z), together(solved)
        left = jnp.where(inside, 0.0, jnp.where(lane < base, -w_rows, w_rows))
        update = product(left, z_rows)
        rows = [
            solved_rows if h == g else jnp.where(inside, 0.0, rows[h]) - update[8 * h : 8 * h + 8, :]
            for h in range(16)
        ]
        if more:
            rows[g + 1] = ahead
    return jnp.concatenate(rows, 0)


def kernel(
    tokens_all,
    inputs_ref, grads_ref, plan_ref, result,
    data, given, taken, sums, in_y, in_z, next_z, next_y, last_in, part_z, part_y, last, own,
    load_sem, core_send, core_recv, y_send, y_recv, z_send, z_recv,
    z2_send, z2_recv, y2_send, y2_recv, x_send, x_recv,
    a1_send, a1_recv, b1_send, b1_recv, a2_send, a2_recv, b2_send, b2_recv,
    c_send, c_recv, own_sem,
):
    section = lax.axis_index("section")
    dp = lax.axis_index("dp")
    z, y, x, core = dp // 16, (dp // 4) % 4, (dp // 2) % 2, dp % 2

    def device(dz=0, dy=0, dx=0, dc=0):
        there = (((z + dz) % 4) * 4 + (y + dy) % 4) * 4 + ((x + dx) % 2) * 2 + (core + dc) % 2
        return (section, there)

    def pair_of(dy, dz):
        return ((y + dy) % 4) * 4 + (z + dz) % 4

    def load(ref, half, slot):
        pair = pair_of(*ORDER[slot])
        return pltpu.make_async_copy(
            ref.at[0, :, :, pl.ds(pl.multiple_of(pair * 256, 256), 256)],
            data.at[half, slot],
            load_sem.at[half, slot],
        )

    partners = [device(dc=1)]
    partners += [device(dy=d) for d in (1, 2, 3)] + [device(dz=d) for d in (1, 2, 3)]
    partners += [device(dx=1)]
    barrier = pltpu.get_barrier_semaphore()
    for partner in partners:
        pl.semaphore_signal(barrier, inc=1, device_id=partner, device_id_type=MESH)

    for mine, refs in ((0, (grads_ref, inputs_ref)), (1, (inputs_ref, grads_ref))):

        @pl.when(core == mine)
        def _():
            for half, first in TURNS:
                for slot in range(first, first + GROUP):
                    load(refs[half], half, slot).start()

    row = lax.broadcasted_iota(jnp.int32, (HEAD, HEAD), 0)
    col = lax.broadcasted_iota(jnp.int32, (HEAD, HEAD), 1)

    def gram(half, slot):
        pair = pair_of(*ORDER[slot])
        whose = core if half else 1 - core
        factor = whose * 32 + pair * 2
        whole = data[half, slot].reshape(-1, 256)
        blocks = []
        for b in range(2):
            newest = plan_ref[0, 1, factor + b]
            own = slice(b * HEAD, (b + 1) * HEAD)
            right = [data[half, slot, 0, :, own]]
            for m in range(1, MICRO):
                kept = jnp.minimum(jnp.maximum(newest - (m - 1), 0), 1).astype(jnp.float32)
                kept = jnp.full((1, HEAD), kept, jnp.float32).astype(jnp.bfloat16)
                right.append(data[half, slot, m, :, own] * kept)
            blocks.append(
                lax.dot_general(
                    whole[:, own],
                    jnp.concatenate(right, 0),
                    (((0,), (0,)), ((), ())),
                    preferred_element_type=jnp.float32,
                )
            )
        packed = jnp.where(row >= col, blocks[0], blocks[1])
        diagonal = jnp.where(row == col, blocks[1], 0.0)
        return packed, jnp.sum(diagonal.reshape(16, 8, HEAD), axis=0)

    def remote(src, dst, send, recv, to):
        return pltpu.make_async_remote_copy(
            src_ref=src, dst_ref=dst, send_sem=send, recv_sem=recv, device_id=to, device_id_type=MESH
        )

    sent = []

    def start(copy):
        copy.start()
        sent.append(copy)

    def core_copy(slot):
        return remote(given.at[slot], taken.at[slot], core_send.at[slot], core_recv.at[slot], device(dc=1))

    def y_copy(dy, dz):
        slot = SLOT[dy, dz]
        i = (dy - 1) * 4 + dz
        return remote(sums.at[slot, 0:CUT], in_y.at[i], y_send.at[i], y_recv.at[i], device(dy=dy))

    def z_copy(dy, dz):
        slot = SLOT[dy, dz]
        i = (dz - 1) * 4 + dy
        return remote(sums.at[slot, CUT:PACK], in_z.at[i], z_send.at[i], z_recv.at[i], device(dz=dz))

    def work_other(first):
        for slot in range(first, first + GROUP):
            load(inputs_ref, 0, slot).wait()
        for slot in range(first, first + GROUP):
            packed, diagonal = gram(0, slot)
            given[slot, 0:HEAD, :] = packed
            given[slot, HEAD:PACK, :] = diagonal
        if first == 0:
            pl.semaphore_wait(barrier, len(partners))
        for slot in range(first, first + GROUP):
            start(core_copy(slot))

    def work_own(first):
        for slot in range(first, first + GROUP):
            load(inputs_ref, 1, slot).wait()
            core_copy(slot).wait_recv()
        for slot in range(first, first + GROUP):
            packed, diagonal = gram(1, slot)
            sums[slot, 0:HEAD, :] = packed + taken[slot, 0:HEAD, :]
            sums[slot, HEAD:PACK, :] = diagonal + taken[slot, HEAD:PACK, :]
        for slot in range(first, first + GROUP):
            dy, dz = ORDER[slot]
            if dy:
                start(y_copy(dy, dz))
            if dz:
                start(z_copy(dy, dz))

    for half, first in TURNS:
        (work_own if half else work_other)(first)

    def z2_copy(dz):
        return remote(part_z.at[dz], next_z.at[dz - 1], z2_send.at[dz - 1], z2_recv.at[dz - 1], device(dz=dz))

    def y2_copy(dy):
        return remote(part_y.at[dy], next_y.at[dy - 1], y2_send.at[dy - 1], y2_recv.at[dy - 1], device(dy=dy))

    for d in (2, 1, 3, 0):
        for o in (1, 2, 3):
            y_copy(o, d).wait_recv()
        part_z[d] = (sums[SLOT[0, d], 0:CUT] + in_y[d]) + (in_y[4 + d] + in_y[8 + d])
        if d:
            start(z2_copy(d))
        for o in (1, 2, 3):
            z_copy(d, o).wait_recv()
        part_y[d] = (sums[SLOT[d, 0], CUT:PACK] + in_z[d]) + (in_z[4 + d] + in_z[8 + d])
        if d:
            start(y2_copy(d))

    def x_copy(i, where):
        return remote(last.at[where], last_in.at[where], x_send.at[i], x_recv.at[i], device(dx=1))

    for d in (1, 3, 2):
        z2_copy(d).wait_recv()
    last[0:CUT] = (part_z[0] + next_z[0]) + (next_z[1] + next_z[2])
    start(x_copy(0, slice(0, CUT)))
    for d in (1, 3, 2):
        y2_copy(d).wait_recv()
    last[CUT:PACK] = (part_y[0] + next_y[0]) + (next_y[1] + next_y[2])
    start(x_copy(1, slice(CUT, PACK)))
    x_copy(0, slice(0, CUT)).wait_recv()
    x_copy(1, slice(CUT, PACK)).wait_recv()

    packed = last[0:HEAD] + last_in[0:HEAD]
    diagonal = jnp.sum(last[HEAD:PACK] + last_in[HEAD:PACK], axis=0, keepdims=True)
    second = x.astype(jnp.float32)
    triangle = jnp.where((row - col) * (1 - 2 * x) > 0, packed, 0.0)
    diagonal = second * diagonal + (1.0 - second) * packed
    total = triangle + triangle.T + jnp.where(row == col, diagonal, 0.0)
    newest = plan_ref[0, 1, core * 32 + pair_of(0, 0) * 2 + x]
    count = jnp.full((1, HEAD), (newest + 1).astype(jnp.float32), jnp.float32) * float(tokens_all)
    damped = total / count + jnp.where(row == col, DAMPING, 0.0)
    inverse = invert(damped)
    own[...] = inverse.astype(jnp.bfloat16)
    place = pltpu.make_async_copy(own, result.at[core, y, z, x], own_sem.at[0])
    place.start()

    def a1_copy(dx, dy):
        i = dx * 4 + dy - 1
        here = result.at[core, y, z, x, 0:CUT]
        return remote(own.at[0:CUT], here, a1_send.at[i], a1_recv.at[i], device(dx=dx, dy=dy))

    def b1_copy(dx, dz):
        i = dx * 4 + dz - 1
        here = result.at[core, y, z, x, CUT:HEAD]
        return remote(own.at[CUT:HEAD], here, b1_send.at[i], b1_recv.at[i], device(dx=dx, dz=dz))

    def a1_arrival(dx, dy):
        i = dx * 4 + dy - 1
        here = result.at[core, (y - dy) % 4, z, (x + dx) % 2, 0:CUT]
        return remote(here, here, a1_send.at[i], a1_recv.at[i], device(dx=dx, dy=dy))

    def b1_arrival(dx, dz):
        i = dx * 4 + dz - 1
        here = result.at[core, y, (z - dz) % 4, (x + dx) % 2, CUT:HEAD]
        return remote(here, here, b1_send.at[i], b1_recv.at[i], device(dx=dx, dz=dz))

    def a2_copy(dx, dy, dz):
        i = (dx * 4 + dy) * 3 + dz - 1
        here = result.at[core, (y - dy) % 4, z, (x + dx) % 2, 0:CUT]
        src = here if dx or dy else own.at[0:CUT]
        return remote(src, here, a2_send.at[i], a2_recv.at[i], device(dz=dz))

    def a2_arrival(dx, dy, dz):
        i = (dx * 4 + dy) * 3 + dz - 1
        here = result.at[core, (y - dy) % 4, (z - dz) % 4, (x + dx) % 2, 0:CUT]
        return remote(here, here, a2_send.at[i], a2_recv.at[i], device(dz=dz))

    def b2_copy(dx, dz, dy):
        i = (dx * 4 + dz) * 3 + dy - 1
        here = result.at[core, y, (z - dz) % 4, (x + dx) % 2, CUT:HEAD]
        src = here if dx or dz else own.at[CUT:HEAD]
        return remote(src, here, b2_send.at[i], b2_recv.at[i], device(dy=dy))

    def b2_arrival(dx, dz, dy):
        i = (dx * 4 + dz) * 3 + dy - 1
        here = result.at[core, (y - dy) % 4, (z - dz) % 4, (x + dx) % 2, CUT:HEAD]
        return remote(here, here, b2_send.at[i], b2_recv.at[i], device(dy=dy))

    first_steps = [(0, 2), (1, 2), (1, 0), (1, 1), (1, 3), (0, 1), (0, 3)]
    for dx, d in first_steps:
        start(a1_copy(dx, d))
        start(b1_copy(dx, d))
    for o in (2, 1, 3):
        start(a2_copy(0, 0, o))
        start(b2_copy(0, 0, o))
    arrivals = [(0, 1), (0, 3), (0, 2), (1, 0), (1, 1), (1, 3), (1, 2)]
    for dx, d in arrivals:
        a1_arrival(dx, d).wait_recv()
        for o in (2, 1, 3):
            start(a2_copy(dx, d, o))
        b1_arrival(dx, d).wait_recv()
        for o in (2, 1, 3):
            start(b2_copy(dx, d, o))
    place.wait()

    def a3_copy(whose, dz):
        here = result.at[whose, :, (z - dz) % 4, :, 0:CUT]
        return remote(here, here, c_send.at[dz], c_recv.at[dz], device(dc=1))

    def b3_copy(whose, dy):
        here = result.at[whose, (y - dy) % 4, :, :, CUT:HEAD]
        return remote(here, here, c_send.at[4 + dy], c_recv.at[4 + dy], device(dc=1))

    start(a3_copy(core, 0))
    start(b3_copy(core, 0))
    for d in (1, 3, 2):
        for dx, o in [(0, 0)] + arrivals:
            a2_arrival(dx, o, d).wait_recv()
        start(a3_copy(core, d))
        for dx, o in [(0, 0)] + arrivals:
            b2_arrival(dx, o, d).wait_recv()
        start(b3_copy(core, d))
    for d in range(4):
        a3_copy(1 - core, d).wait_recv()
        b3_copy(1 - core, d).wait_recv()
    for copy in sent:
        copy.wait_send()


def shards(inputs, query_grads, plan):
    micro, tokens = inputs.shape[1], inputs.shape[2]
    members = lax.axis_size("dp")
    dma = pltpu.SemaphoreType.DMA
    f32, bf16 = jnp.float32, jnp.bfloat16
    vmem = pltpu.VMEM
    result = pl.pallas_call(
        functools.partial(kernel, tokens * members),
        out_shape=pltpu.VMEM((2, 4, 4, 2, HEAD, HEAD), bf16),
        in_specs=[
            pl.BlockSpec(memory_space=pl.ANY),
            pl.BlockSpec(memory_space=pl.ANY),
            pl.BlockSpec(memory_space=pltpu.SMEM),
        ],
        out_specs=pl.BlockSpec(memory_space=pl.ANY),
        scratch_shapes=[
            vmem((2, PAIRS, micro, tokens, 256), bf16),
            vmem((PAIRS, PACK, HEAD), f32),
            vmem((PAIRS, PACK, HEAD), f32),
            vmem((PAIRS, PACK, HEAD), f32),
            vmem((12, CUT, HEAD), f32),
            vmem((12, PACK - CUT, HEAD), f32),
            vmem((3, CUT, HEAD), f32),
            vmem((3, PACK - CUT, HEAD), f32),
            vmem((PACK, HEAD), f32),
            vmem((4, CUT, HEAD), f32),
            vmem((4, PACK - CUT, HEAD), f32),
            vmem((PACK, HEAD), f32),
            vmem((HEAD, HEAD), bf16),
            dma((2, PAIRS)),
            dma((PAIRS,)), dma((PAIRS,)),
            dma((12,)), dma((12,)), dma((12,)), dma((12,)),
            dma((3,)), dma((3,)), dma((3,)), dma((3,)),
            dma((2,)), dma((2,)),
            dma((7,)), dma((7,)), dma((7,)), dma((7,)),
            dma((24,)), dma((24,)), dma((24,)), dma((24,)),
            dma((8,)), dma((8,)),
            dma((1,)),
        ],
        compiler_params=pltpu.CompilerParams(
            collective_id=0, has_side_effects=True, vmem_limit_bytes=54 << 20
        ),
        name="factor_inverses",
    )(inputs, query_grads, plan.transpose(0, 2, 1))
    return result.reshape(1, 64, HEAD, HEAD)


def solution(mesh):
    in_specs = (
        P("section", None, "dp", None),
        P("section", None, "dp", None),
        P("section", None, None),
    )
    out_specs = P("section", None, None, None)
    return jax.shard_map(shards, mesh=mesh, in_specs=in_specs, out_specs=out_specs, check_vma=False)
```

```python
import functools

import jax
import jax.numpy as jnp
from jax import lax
from jax.experimental import pallas as pl
from jax.experimental.pallas import tpu as pltpu
from jax.sharding import PartitionSpec as P

HEAD = 128
DAMPING = 0.3
MICRO = 4
PAIRS = 16
PACK = 136
CUT = 64
MESH = pl.DeviceIdType.MESH

ORDER = (
    (2, 2), (2, 1), (1, 2),
    (2, 3), (3, 2), (1, 1),
    (1, 3), (3, 1), (3, 3),
    (2, 0), (0, 2), (1, 0), (0, 1),
    (3, 0), (0, 3), (0, 0),
)
SLOT = {offset: slot for slot, offset in enumerate(ORDER)}
GROUPS = (range(0, 3), range(3, 6), range(6, 9), range(9, 13), range(13, 16))
TURNS = tuple(
    (half, GROUPS[group])
    for half, group in ((0, 0), (0, 1), (1, 0), (0, 2), (1, 1), (0, 3), (1, 2), (0, 4), (1, 3), (1, 4))
)

def split3(x):
    high = x.astype(jnp.bfloat16)
    x = x - high.astype(jnp.float32)
    middle = x.astype(jnp.bfloat16)
    x = x - middle.astype(jnp.float32)
    return high, middle, x.astype(jnp.bfloat16)


def product(a, b):
    ah, am, al = split3(a)
    bh, bm, bl = split3(b)
    left = jnp.concatenate([ah, ah, am, ah, al, am], 0)
    right = jnp.concatenate([bh, bm, bh, bl, bh, bm], 0)
    return lax.dot_general(left, right, (((0,), (0,)), ((), ())), preferred_element_type=jnp.float32)


def spread(x):
    return jnp.broadcast_to(x, (8, HEAD))


def invert(matrix):
    lane = lax.broadcasted_iota(jnp.int32, (8, HEAD), 1)
    sub = lax.broadcasted_iota(jnp.int32, (8, HEAD), 0)
    rows = [matrix[8 * g : 8 * g + 8, :] for g in range(16)]
    for g in range(16):
        base = 8 * g
        panel = rows[g]
        inside = (lane >= base) & (lane < base + 8)
        columns = [spread(panel[:, base + j : base + j + 1]) for j in range(8)]
        a = {(i, j): spread(columns[j][i : i + 1, :]) for i in range(8) for j in range(i, 8)}
        start = jnp.where(inside, jnp.where(lane - base == sub, 1.0, 0.0), panel)
        w = [spread(start[j : j + 1, :]) for j in range(8)]
        more = g + 1 < 16
        if more:
            following = rows[g + 1]
            c = [spread(following[:, base + j : base + j + 1]) for j in range(8)]
        low = {}
        inverse_d = [None] * 8
        for i in (0, 2, 4, 6):
            p, q, r = a[i, i], a[i, i + 1], a[i + 1, i + 1]
            d0 = 1.0 / p
            d1 = p * (1.0 / (p * r - q * q))
            l10 = q * d0
            inverse_d[i], inverse_d[i + 1] = d0, d1
            low[i + 1, i] = l10
            e0 = {j: a[i, j] for j in range(i + 2, 8)}
            e1 = {j: a[i + 1, j] - l10 * a[i, j] for j in range(i + 2, 8)}
            for j in range(i + 2, 8):
                low[j, i], low[j, i + 1] = e0[j] * d0, e1[j] * d1
            for j in range(i + 2, 8):
                for m in range(j, 8):
                    a[j, m] = a[j, m] - (low[j, i] * e0[m] + low[j, i + 1] * e1[m])
            w[i + 1] = w[i + 1] - l10 * w[i]
            for j in range(i + 2, 8):
                w[j] = w[j] - (low[j, i] * w[i] + low[j, i + 1] * w[i + 1])
            if more:
                c[i + 1] = c[i + 1] - l10 * c[i]
                for j in range(i + 2, 8):
                    c[j] = c[j] - (low[j, i] * c[i] + low[j, i + 1] * c[i + 1])
        z = [inverse_d[j] * w[j] for j in range(8)]
        if more:
            t = [c[j] * z[j] for j in range(8)]
            t = ((t[0] + t[1]) + (t[2] + t[3])) + ((t[4] + t[5]) + (t[6] + t[7]))
            ahead = jnp.where(inside, 0.0, following) - t
        solved = list(z)
        for j in range(7, -1, -1):
            for i in range(j):
                solved[i] = solved[i] - low[j, i] * solved[j]

        def together(parts):
            whole = parts[7]
            for i in range(7):
                whole = jnp.where(sub == i, parts[i], whole)
            return whole

        w_rows, z_rows, solved_rows = together(w), together(z), together(solved)
        left = jnp.where(inside, 0.0, jnp.where(lane < base, -w_rows, w_rows))
        update = product(left, z_rows)
        rows = [
            solved_rows if h == g else jnp.where(inside, 0.0, rows[h]) - update[8 * h : 8 * h + 8, :]
            for h in range(16)
        ]
        if more:
            rows[g + 1] = ahead
    return jnp.concatenate(rows, 0)


def kernel(
    tokens_all,
    inputs_ref, grads_ref, plan_ref, result,
    data, given, taken, sums, in_y, in_z, next_z, next_y, last_in, part_z, part_y, last, own,
    load_sem, core_send, core_recv, y_send, y_recv, z_send, z_recv,
    z2_send, z2_recv, y2_send, y2_recv, x_send, x_recv,
    a1_send, a1_recv, b1_send, b1_recv, a2_send, a2_recv, b2_send, b2_recv,
    c_send, c_recv, own_sem,
):
    section = lax.axis_index("section")
    dp = lax.axis_index("dp")
    z, y, x, core = dp // 16, (dp // 4) % 4, (dp // 2) % 2, dp % 2

    def device(dz=0, dy=0, dx=0, dc=0):
        there = (((z + dz) % 4) * 4 + (y + dy) % 4) * 4 + ((x + dx) % 2) * 2 + (core + dc) % 2
        return (section, there)

    def pair_of(dy, dz):
        return ((y + dy) % 4) * 4 + (z + dz) % 4

    def load(ref, half, slot):
        pair = pair_of(*ORDER[slot])
        return pltpu.make_async_copy(
            ref.at[0, :, :, pl.ds(pl.multiple_of(pair * 256, 256), 256)],
            data.at[half, slot],
            load_sem.at[half, slot],
        )

    partners = [device(dc=1)]
    partners += [device(dy=d) for d in (1, 2, 3)] + [device(dz=d) for d in (1, 2, 3)]
    partners += [device(dx=1)]
    barrier = pltpu.get_barrier_semaphore()
    for partner in partners:
        pl.semaphore_signal(barrier, inc=1, device_id=partner, device_id_type=MESH)

    for mine, refs in ((0, (grads_ref, inputs_ref)), (1, (inputs_ref, grads_ref))):

        @pl.when(core == mine)
        def _():
            for half, slots in TURNS:
                for slot in slots:
                    load(refs[half], half, slot).start()

    row = lax.broadcasted_iota(jnp.int32, (HEAD, HEAD), 0)
    col = lax.broadcasted_iota(jnp.int32, (HEAD, HEAD), 1)

    def gram(half, slot):
        pair = pair_of(*ORDER[slot])
        whose = core if half else 1 - core
        factor = whose * 32 + pair * 2
        whole = data[half, slot].reshape(-1, 256)
        blocks = []
        for b in range(2):
            newest = plan_ref[0, 1, factor + b]
            own = slice(b * HEAD, (b + 1) * HEAD)
            right = [data[half, slot, 0, :, own]]
            for m in range(1, MICRO):
                kept = jnp.minimum(jnp.maximum(newest - (m - 1), 0), 1).astype(jnp.float32)
                kept = jnp.full((1, HEAD), kept, jnp.float32).astype(jnp.bfloat16)
                right.append(data[half, slot, m, :, own] * kept)
            blocks.append(
                lax.dot_general(
                    whole[:, own],
                    jnp.concatenate(right, 0),
                    (((0,), (0,)), ((), ())),
                    preferred_element_type=jnp.float32,
                )
            )
        packed = jnp.where(row >= col, blocks[0], blocks[1])
        diagonal = jnp.where(row == col, blocks[1], 0.0)
        return packed, jnp.sum(diagonal.reshape(16, 8, HEAD), axis=0)

    def remote(src, dst, send, recv, to):
        return pltpu.make_async_remote_copy(
            src_ref=src, dst_ref=dst, send_sem=send, recv_sem=recv, device_id=to, device_id_type=MESH
        )

    sent = []

    def start(copy):
        copy.start()
        sent.append(copy)

    def core_copy(slot):
        return remote(given.at[slot], taken.at[slot], core_send.at[slot], core_recv.at[slot], device(dc=1))

    def y_copy(dy, dz):
        slot = SLOT[dy, dz]
        i = (dy - 1) * 4 + dz
        return remote(sums.at[slot, 0:CUT], in_y.at[i], y_send.at[i], y_recv.at[i], device(dy=dy))

    def z_copy(dy, dz):
        slot = SLOT[dy, dz]
        i = (dz - 1) * 4 + dy
        return remote(sums.at[slot, CUT:PACK], in_z.at[i], z_send.at[i], z_recv.at[i], device(dz=dz))

    def work_other(slots):
        for slot in slots:
            load(inputs_ref, 0, slot).wait()
        for slot in slots:
            packed, diagonal = gram(0, slot)
            given[slot, 0:HEAD, :] = packed
            given[slot, HEAD:PACK, :] = diagonal
        if slots[0] == 0:
            pl.semaphore_wait(barrier, len(partners))
        for slot in slots:
            start(core_copy(slot))

    def work_own(slots):
        for slot in slots:
            load(inputs_ref, 1, slot).wait()
            core_copy(slot).wait_recv()
        for slot in slots:
            packed, diagonal = gram(1, slot)
            sums[slot, 0:HEAD, :] = packed + taken[slot, 0:HEAD, :]
            sums[slot, HEAD:PACK, :] = diagonal + taken[slot, HEAD:PACK, :]
        for slot in slots:
            dy, dz = ORDER[slot]
            if dy:
                start(y_copy(dy, dz))
            if dz:
                start(z_copy(dy, dz))

    for half, slots in TURNS:
        (work_own if half else work_other)(slots)

    def z2_copy(dz):
        return remote(part_z.at[dz], next_z.at[dz - 1], z2_send.at[dz - 1], z2_recv.at[dz - 1], device(dz=dz))

    def y2_copy(dy):
        return remote(part_y.at[dy], next_y.at[dy - 1], y2_send.at[dy - 1], y2_recv.at[dy - 1], device(dy=dy))

    for d in (2, 1, 3, 0):
        for o in (1, 2, 3):
            y_copy(o, d).wait_recv()
        part_z[d] = (sums[SLOT[0, d], 0:CUT] + in_y[d]) + (in_y[4 + d] + in_y[8 + d])
        if d:
            start(z2_copy(d))
        for o in (1, 2, 3):
            z_copy(d, o).wait_recv()
        part_y[d] = (sums[SLOT[d, 0], CUT:PACK] + in_z[d]) + (in_z[4 + d] + in_z[8 + d])
        if d:
            start(y2_copy(d))

    def x_copy(i, where):
        return remote(last.at[where], last_in.at[where], x_send.at[i], x_recv.at[i], device(dx=1))

    for d in (1, 3, 2):
        z2_copy(d).wait_recv()
    last[0:CUT] = (part_z[0] + next_z[0]) + (next_z[1] + next_z[2])
    start(x_copy(0, slice(0, CUT)))
    for d in (1, 3, 2):
        y2_copy(d).wait_recv()
    last[CUT:PACK] = (part_y[0] + next_y[0]) + (next_y[1] + next_y[2])
    start(x_copy(1, slice(CUT, PACK)))
    x_copy(0, slice(0, CUT)).wait_recv()
    x_copy(1, slice(CUT, PACK)).wait_recv()

    packed = last[0:HEAD] + last_in[0:HEAD]
    diagonal = jnp.sum(last[HEAD:PACK] + last_in[HEAD:PACK], axis=0, keepdims=True)
    second = x.astype(jnp.float32)
    triangle = jnp.where((row - col) * (1 - 2 * x) > 0, packed, 0.0)
    diagonal = second * diagonal + (1.0 - second) * packed
    total = triangle + triangle.T + jnp.where(row == col, diagonal, 0.0)
    newest = plan_ref[0, 1, core * 32 + pair_of(0, 0) * 2 + x]
    count = jnp.full((1, HEAD), (newest + 1).astype(jnp.float32), jnp.float32) * float(tokens_all)
    damped = total / count + jnp.where(row == col, DAMPING, 0.0)
    inverse = invert(damped)
    own[...] = inverse.astype(jnp.bfloat16)
    place = pltpu.make_async_copy(own, result.at[core, y, z, x], own_sem.at[0])
    place.start()

    def a1_copy(dx, dy):
        i = dx * 4 + dy - 1
        here = result.at[core, y, z, x, 0:CUT]
        return remote(own.at[0:CUT], here, a1_send.at[i], a1_recv.at[i], device(dx=dx, dy=dy))

    def b1_copy(dx, dz):
        i = dx * 4 + dz - 1
        here = result.at[core, y, z, x, CUT:HEAD]
        return remote(own.at[CUT:HEAD], here, b1_send.at[i], b1_recv.at[i], device(dx=dx, dz=dz))

    def a1_arrival(dx, dy):
        i = dx * 4 + dy - 1
        here = result.at[core, (y - dy) % 4, z, (x + dx) % 2, 0:CUT]
        return remote(here, here, a1_send.at[i], a1_recv.at[i], device(dx=dx, dy=dy))

    def b1_arrival(dx, dz):
        i = dx * 4 + dz - 1
        here = result.at[core, y, (z - dz) % 4, (x + dx) % 2, CUT:HEAD]
        return remote(here, here, b1_send.at[i], b1_recv.at[i], device(dx=dx, dz=dz))

    def a2_copy(dx, dy, dz):
        i = (dx * 4 + dy) * 3 + dz - 1
        here = result.at[core, (y - dy) % 4, z, (x + dx) % 2, 0:CUT]
        src = here if dx or dy else own.at[0:CUT]
        return remote(src, here, a2_send.at[i], a2_recv.at[i], device(dz=dz))

    def a2_arrival(dx, dy, dz):
        i = (dx * 4 + dy) * 3 + dz - 1
        here = result.at[core, (y - dy) % 4, (z - dz) % 4, (x + dx) % 2, 0:CUT]
        return remote(here, here, a2_send.at[i], a2_recv.at[i], device(dz=dz))

    def b2_copy(dx, dz, dy):
        i = (dx * 4 + dz) * 3 + dy - 1
        here = result.at[core, y, (z - dz) % 4, (x + dx) % 2, CUT:HEAD]
        src = here if dx or dz else own.at[CUT:HEAD]
        return remote(src, here, b2_send.at[i], b2_recv.at[i], device(dy=dy))

    def b2_arrival(dx, dz, dy):
        i = (dx * 4 + dz) * 3 + dy - 1
        here = result.at[core, (y - dy) % 4, (z - dz) % 4, (x + dx) % 2, CUT:HEAD]
        return remote(here, here, b2_send.at[i], b2_recv.at[i], device(dy=dy))

    first_steps = [(0, 2), (1, 2), (1, 0), (1, 1), (1, 3), (0, 1), (0, 3)]
    for dx, d in first_steps:
        start(a1_copy(dx, d))
        start(b1_copy(dx, d))
    for o in (2, 1, 3):
        start(a2_copy(0, 0, o))
        start(b2_copy(0, 0, o))
    arrivals = [(0, 1), (0, 3), (0, 2), (1, 0), (1, 1), (1, 3), (1, 2)]
    for dx, d in arrivals:
        a1_arrival(dx, d).wait_recv()
        for o in (2, 1, 3):
            start(a2_copy(dx, d, o))
        b1_arrival(dx, d).wait_recv()
        for o in (2, 1, 3):
            start(b2_copy(dx, d, o))
    place.wait()

    def a3_copy(whose, dx, dy):
        i = dx * 4 + dy
        here = result.at[whose, (y - dy) % 4, :, (x + dx) % 2, 0:CUT]
        return remote(here, here, c_send.at[0, i], c_recv.at[0, i], device(dc=1))

    def b3_copy(whose, dx, dz):
        i = dx * 4 + dz
        here = result.at[whose, :, (z - dz) % 4, (x + dx) % 2, CUT:HEAD]
        return remote(here, here, c_send.at[1, i], c_recv.at[1, i], device(dc=1))

    ways = [(0, 0)] + arrivals
    for dx, d in ways:
        for o in (1, 3, 2):
            a2_arrival(dx, d, o).wait_recv()
        start(a3_copy(core, dx, d))
        for o in (1, 3, 2):
            b2_arrival(dx, d, o).wait_recv()
        start(b3_copy(core, dx, d))
    for dx, d in ways:
        a3_copy(1 - core, dx, d).wait_recv()
        b3_copy(1 - core, dx, d).wait_recv()
    for copy in sent:
        copy.wait_send()


def shards(inputs, query_grads, plan):
    micro, tokens = inputs.shape[1], inputs.shape[2]
    members = lax.axis_size("dp")
    dma = pltpu.SemaphoreType.DMA
    f32, bf16 = jnp.float32, jnp.bfloat16
    vmem = pltpu.VMEM
    result = pl.pallas_call(
        functools.partial(kernel, tokens * members),
        out_shape=pltpu.VMEM((2, 4, 4, 2, HEAD, HEAD), bf16),
        in_specs=[
            pl.BlockSpec(memory_space=pl.ANY),
            pl.BlockSpec(memory_space=pl.ANY),
            pl.BlockSpec(memory_space=pltpu.SMEM),
        ],
        out_specs=pl.BlockSpec(memory_space=pl.ANY),
        scratch_shapes=[
            vmem((2, PAIRS, micro, tokens, 256), bf16),
            vmem((PAIRS, PACK, HEAD), f32),
            vmem((PAIRS, PACK, HEAD), f32),
            vmem((PAIRS, PACK, HEAD), f32),
            vmem((12, CUT, HEAD), f32),
            vmem((12, PACK - CUT, HEAD), f32),
            vmem((3, CUT, HEAD), f32),
            vmem((3, PACK - CUT, HEAD), f32),
            vmem((PACK, HEAD), f32),
            vmem((4, CUT, HEAD), f32),
            vmem((4, PACK - CUT, HEAD), f32),
            vmem((PACK, HEAD), f32),
            vmem((HEAD, HEAD), bf16),
            dma((2, PAIRS)),
            dma((PAIRS,)), dma((PAIRS,)),
            dma((12,)), dma((12,)), dma((12,)), dma((12,)),
            dma((3,)), dma((3,)), dma((3,)), dma((3,)),
            dma((2,)), dma((2,)),
            dma((7,)), dma((7,)), dma((7,)), dma((7,)),
            dma((24,)), dma((24,)), dma((24,)), dma((24,)),
            dma((2, 8)), dma((2, 8)),
            dma((1,)),
        ],
        compiler_params=pltpu.CompilerParams(
            collective_id=0, has_side_effects=True, vmem_limit_bytes=54 << 20
        ),
        name="factor_inverses",
    )(inputs, query_grads, plan.transpose(0, 2, 1))
    return result.reshape(1, 64, HEAD, HEAD)


def solution(mesh):
    in_specs = (
        P("section", None, "dp", None),
        P("section", None, "dp", None),
        P("section", None, None),
    )
    out_specs = P("section", None, None, None)
    return jax.shard_map(shards, mesh=mesh, in_specs=in_specs, out_specs=out_specs, check_vma=False)
```

```python
import functools

import jax
import jax.numpy as jnp
from jax import lax
from jax.experimental import pallas as pl
from jax.experimental.pallas import tpu as pltpu
from jax.sharding import PartitionSpec as P

HEAD = 128
DAMPING = 0.3
MICRO = 4
PAIRS = 16
PACK = 136
CUT = 64
MESH = pl.DeviceIdType.MESH

ORDER = (
    (2, 2), (2, 1), (1, 2),
    (2, 3), (3, 2), (1, 1),
    (1, 3), (3, 1), (3, 3),
    (2, 0), (0, 2), (1, 0), (0, 1),
    (3, 0), (0, 3), (0, 0),
)
SLOT = {offset: slot for slot, offset in enumerate(ORDER)}
GROUPS = (range(0, 3), range(3, 6), range(6, 9), range(9, 13), range(13, 16))
TURNS = tuple(
    (half, GROUPS[group])
    for half, group in ((0, 0), (0, 1), (1, 0), (0, 2), (1, 1), (0, 3), (1, 2), (0, 4), (1, 3), (1, 4))
)

def split3(x):
    high = x.astype(jnp.bfloat16)
    x = x - high.astype(jnp.float32)
    middle = x.astype(jnp.bfloat16)
    x = x - middle.astype(jnp.float32)
    return high, middle, x.astype(jnp.bfloat16)


def product(a, b):
    ah, am, al = split3(a)
    bh, bm, bl = split3(b)
    left = jnp.concatenate([ah, ah, am, ah, al, am], 0)
    right = jnp.concatenate([bh, bm, bh, bl, bh, bm], 0)
    return lax.dot_general(left, right, (((0,), (0,)), ((), ())), preferred_element_type=jnp.float32)


def spread(x):
    return jnp.broadcast_to(x, (8, HEAD))


AHEAD = 3


def invert(matrix, spot):
    lane = lax.broadcasted_iota(jnp.int32, (8, HEAD), 1)
    sub = lax.broadcasted_iota(jnp.int32, (8, HEAD), 0)
    rows = [matrix[8 * g : 8 * g + 8, :] for g in range(16)]
    for g in range(16):
        base = 8 * g
        panel = rows[g]
        inside = (lane >= base) & (lane < base + 8)
        start = jnp.where(inside, jnp.where(lane - base == sub, 1.0, 0.0), panel)
        here = (g % 2) * 9
        for j in range(8):
            spot[here + j] = spread(panel[:, base + j : base + j + 1])
        spot[here + 8] = start
        a = {(i, j): spread(spot[here + j, pl.ds(i, 1), :]) for i in range(8) for j in range(i, 8)}
        w = [spread(spot[here + 8, pl.ds(j, 1), :]) for j in range(8)]
        following = range(g + 1, min(16, g + 1 + AHEAD))
        c = {h: [spread(rows[h][:, base + j : base + j + 1]) for j in range(8)] for h in following}
        low = {}
        inverse_d = [None] * 8
        for i in (0, 2, 4, 6):
            p, q, r = a[i, i], a[i, i + 1], a[i + 1, i + 1]
            d0 = 1.0 / p
            d1 = p * (1.0 / (p * r - q * q))
            l10 = q * d0
            inverse_d[i], inverse_d[i + 1] = d0, d1
            low[i + 1, i] = l10
            e0 = {j: a[i, j] for j in range(i + 2, 8)}
            e1 = {j: a[i + 1, j] - l10 * a[i, j] for j in range(i + 2, 8)}
            for j in range(i + 2, 8):
                low[j, i], low[j, i + 1] = e0[j] * d0, e1[j] * d1
            for j in range(i + 2, 8):
                for m in range(j, 8):
                    a[j, m] = a[j, m] - (low[j, i] * e0[m] + low[j, i + 1] * e1[m])
            for v in [w, *c.values()]:
                v[i + 1] = v[i + 1] - l10 * v[i]
                for j in range(i + 2, 8):
                    v[j] = v[j] - (low[j, i] * v[i] + low[j, i + 1] * v[i + 1])
        z = [inverse_d[j] * w[j] for j in range(8)]
        ahead = {}
        for h in following:
            t = [c[h][j] * z[j] for j in range(8)]
            t = ((t[0] + t[1]) + (t[2] + t[3])) + ((t[4] + t[5]) + (t[6] + t[7]))
            ahead[h] = jnp.where(inside, 0.0, rows[h]) - t
        solved = list(z)
        for j in range(7, -1, -1):
            for i in range(j):
                solved[i] = solved[i] - low[j, i] * solved[j]

        def together(parts):
            whole = parts[7]
            for i in range(7):
                whole = jnp.where(sub == i, parts[i], whole)
            return whole

        w_rows, z_rows, solved_rows = together(w), together(z), together(solved)
        left = jnp.where(inside, 0.0, jnp.where(lane < base, -w_rows, w_rows))
        update = product(left, z_rows)
        rows = [
            solved_rows if h == g else jnp.where(inside, 0.0, rows[h]) - update[8 * h : 8 * h + 8, :]
            for h in range(16)
        ]
        for h in following:
            rows[h] = ahead[h]
    return jnp.concatenate(rows, 0)


def kernel(
    tokens_all,
    inputs_ref, grads_ref, plan_ref, result,
    data, given, taken, sums, in_y, in_z, next_z, next_y, last_in, part_z, part_y, last, own, spot,
    load_sem, core_send, core_recv, y_send, y_recv, z_send, z_recv,
    z2_send, z2_recv, y2_send, y2_recv, x_send, x_recv,
    a1_send, a1_recv, b1_send, b1_recv, a2_send, a2_recv, b2_send, b2_recv,
    c_send, c_recv, own_sem,
):
    section = lax.axis_index("section")
    dp = lax.axis_index("dp")
    z, y, x, core = dp // 16, (dp // 4) % 4, (dp // 2) % 2, dp % 2

    def device(dz=0, dy=0, dx=0, dc=0):
        there = (((z + dz) % 4) * 4 + (y + dy) % 4) * 4 + ((x + dx) % 2) * 2 + (core + dc) % 2
        return (section, there)

    def pair_of(dy, dz):
        return ((y + dy) % 4) * 4 + (z + dz) % 4

    def load(ref, half, slot):
        pair = pair_of(*ORDER[slot])
        return pltpu.make_async_copy(
            ref.at[0, :, :, pl.ds(pl.multiple_of(pair * 256, 256), 256)],
            data.at[half, slot],
            load_sem.at[half, slot],
        )

    partners = [device(dc=1)]
    partners += [device(dy=d) for d in (1, 2, 3)] + [device(dz=d) for d in (1, 2, 3)]
    partners += [device(dx=1)]
    barrier = pltpu.get_barrier_semaphore()
    for partner in partners:
        pl.semaphore_signal(barrier, inc=1, device_id=partner, device_id_type=MESH)

    for mine, refs in ((0, (grads_ref, inputs_ref)), (1, (inputs_ref, grads_ref))):

        @pl.when(core == mine)
        def _():
            for half, slots in TURNS:
                for slot in slots:
                    load(refs[half], half, slot).start()

    row = lax.broadcasted_iota(jnp.int32, (HEAD, HEAD), 0)
    col = lax.broadcasted_iota(jnp.int32, (HEAD, HEAD), 1)
    half_row = lax.broadcasted_iota(jnp.int32, (CUT, HEAD), 0)
    lane = lax.broadcasted_iota(jnp.int32, (CUT, HEAD), 1)

    def gram(half, slot):
        pair = pair_of(*ORDER[slot])
        whose = core if half else 1 - core
        factor = whose * 32 + pair * 2
        whole = data[half, slot].reshape(-1, 256)
        blocks = []
        for b in range(2):
            newest = plan_ref[0, 1, factor + b]
            own = slice(b * HEAD, (b + 1) * HEAD)
            right = [data[half, slot, 0, :, own]]
            for m in range(1, MICRO):
                kept = jnp.minimum(jnp.maximum(newest - (m - 1), 0), 1).astype(jnp.float32)
                kept = jnp.full((1, HEAD), kept, jnp.float32).astype(jnp.bfloat16)
                right.append(data[half, slot, m, :, own] * kept)
            blocks.append(
                lax.dot_general(
                    whole[:, own],
                    jnp.concatenate(right, 0),
                    (((0,), (0,)), ((), ())),
                    preferred_element_type=jnp.float32,
                )
            )
        folded = []
        for block in blocks:
            turned = pltpu.roll(block[CUT:], CUT, 1)
            folded.append(jnp.where(lane <= half_row, block[:CUT], jnp.where(lane >= CUT, block[:CUT], turned)))
        diagonals = jnp.where(lane == half_row, pltpu.roll(blocks[0][CUT:], CUT, 1), 0.0)
        diagonals += jnp.where(lane == half_row + CUT, blocks[1][CUT:], 0.0)
        return folded[0], folded[1], jnp.sum(diagonals.reshape(8, 8, HEAD), axis=0)

    def remote(src, dst, send, recv, to):
        return pltpu.make_async_remote_copy(
            src_ref=src, dst_ref=dst, send_sem=send, recv_sem=recv, device_id=to, device_id_type=MESH
        )

    sent = []

    def start(copy):
        copy.start()
        sent.append(copy)

    def core_copy(slot):
        return remote(given.at[slot], taken.at[slot], core_send.at[slot], core_recv.at[slot], device(dc=1))

    def y_copy(dy, dz):
        slot = SLOT[dy, dz]
        i = (dy - 1) * 4 + dz
        return remote(sums.at[slot, 0:CUT], in_y.at[i], y_send.at[i], y_recv.at[i], device(dy=dy))

    def z_copy(dy, dz):
        slot = SLOT[dy, dz]
        i = (dz - 1) * 4 + dy
        return remote(sums.at[slot, CUT:PACK], in_z.at[i], z_send.at[i], z_recv.at[i], device(dz=dz))

    def work_other(slots):
        for slot in slots:
            load(inputs_ref, 0, slot).wait()
        for slot in slots:
            one, two, diagonals = gram(0, slot)
            given[slot, 0:CUT] = one
            given[slot, CUT:HEAD] = two
            given[slot, HEAD:PACK] = diagonals
        if slots[0] == 0:
            pl.semaphore_wait(barrier, len(partners))
        for slot in slots:
            start(core_copy(slot))

    def work_own(slots):
        for slot in slots:
            load(inputs_ref, 1, slot).wait()
            core_copy(slot).wait_recv()
        for slot in slots:
            one, two, diagonals = gram(1, slot)
            sums[slot, 0:CUT] = one + taken[slot, 0:CUT]
            sums[slot, CUT:HEAD] = two + taken[slot, CUT:HEAD]
            sums[slot, HEAD:PACK] = diagonals + taken[slot, HEAD:PACK]
        for slot in slots:
            dy, dz = ORDER[slot]
            if dy:
                start(y_copy(dy, dz))
            if dz:
                start(z_copy(dy, dz))

    for half, slots in TURNS:
        (work_own if half else work_other)(slots)

    def z2_copy(dz):
        return remote(part_z.at[dz], next_z.at[dz - 1], z2_send.at[dz - 1], z2_recv.at[dz - 1], device(dz=dz))

    def y2_copy(dy):
        return remote(part_y.at[dy], next_y.at[dy - 1], y2_send.at[dy - 1], y2_recv.at[dy - 1], device(dy=dy))

    for d in (2, 1, 3, 0):
        for o in (1, 2, 3):
            y_copy(o, d).wait_recv()
        part_z[d] = (sums[SLOT[0, d], 0:CUT] + in_y[d]) + (in_y[4 + d] + in_y[8 + d])
        if d:
            start(z2_copy(d))
        for o in (1, 2, 3):
            z_copy(d, o).wait_recv()
        part_y[d] = (sums[SLOT[d, 0], CUT:PACK] + in_z[d]) + (in_z[4 + d] + in_z[8 + d])
        if d:
            start(y2_copy(d))

    def rows_of(which):
        return pl.ds(pl.multiple_of(which * CUT, CUT), CUT)

    def x_copy(part):
        src, dst = ((rows_of(1 - x), slice(0, CUT)), (slice(HEAD, PACK), slice(CUT, CUT + 8)))[part]
        return remote(last.at[src], last_in.at[dst], x_send.at[part], x_recv.at[part], device(dx=1))

    for d in (1, 3, 2):
        z2_copy(d).wait_recv()
        y2_copy(d).wait_recv()
    last[0:CUT] = (part_z[0] + next_z[0]) + (next_z[1] + next_z[2])
    last[CUT:PACK] = (part_y[0] + next_y[0]) + (next_y[1] + next_y[2])
    start(x_copy(0))
    start(x_copy(1))
    x_copy(0).wait_recv()
    x_copy(1).wait_recv()

    folded = last[rows_of(x)] + last_in[0:CUT]
    diagonals = jnp.sum(last[HEAD:PACK] + last_in[CUT : CUT + 8], axis=0, keepdims=True)
    second = x.astype(jnp.float32)
    diagonals = second * diagonals + (1.0 - second) * pltpu.roll(jnp.broadcast_to(diagonals, (8, HEAD)), CUT, 1)[0:1]
    unfolded = jnp.concatenate([folded, pltpu.roll(folded, CUT, 1)], 0)
    stored = ((row < CUT) & ((col >= CUT) | (col < row))) | ((row >= CUT) & (col > row))
    triangle = jnp.where(stored, unfolded, 0.0)
    total = triangle + triangle.T + jnp.where(row == col, jnp.where(row < CUT, unfolded, diagonals), 0.0)
    newest = plan_ref[0, 1, core * 32 + pair_of(0, 0) * 2 + x]
    count = jnp.full((1, HEAD), (newest + 1).astype(jnp.float32), jnp.float32) * float(tokens_all)
    damped = total / count + jnp.where(row == col, DAMPING, 0.0)
    inverse = invert(damped, spot)
    own[...] = inverse.astype(jnp.bfloat16)
    place = pltpu.make_async_copy(own, result.at[core, y, z, x], own_sem.at[0])
    place.start()

    def a1_copy(dx, dy):
        i = dx * 4 + dy - 1
        here = result.at[core, y, z, x, 0:CUT]
        return remote(own.at[0:CUT], here, a1_send.at[i], a1_recv.at[i], device(dx=dx, dy=dy))

    def b1_copy(dx, dz):
        i = dx * 4 + dz - 1
        here = result.at[core, y, z, x, CUT:HEAD]
        return remote(own.at[CUT:HEAD], here, b1_send.at[i], b1_recv.at[i], device(dx=dx, dz=dz))

    def a1_arrival(dx, dy):
        i = dx * 4 + dy - 1
        here = result.at[core, (y - dy) % 4, z, (x + dx) % 2, 0:CUT]
        return remote(here, here, a1_send.at[i], a1_recv.at[i], device(dx=dx, dy=dy))

    def b1_arrival(dx, dz):
        i = dx * 4 + dz - 1
        here = result.at[core, y, (z - dz) % 4, (x + dx) % 2, CUT:HEAD]
        return remote(here, here, b1_send.at[i], b1_recv.at[i], device(dx=dx, dz=dz))

    def a2_copy(dx, dy, dz):
        i = (dx * 4 + dy) * 3 + dz - 1
        here = result.at[core, (y - dy) % 4, z, (x + dx) % 2, 0:CUT]
        src = here if dx or dy else own.at[0:CUT]
        return remote(src, here, a2_send.at[i], a2_recv.at[i], device(dz=dz))

    def a2_arrival(dx, dy, dz):
        i = (dx * 4 + dy) * 3 + dz - 1
        here = result.at[core, (y - dy) % 4, (z - dz) % 4, (x + dx) % 2, 0:CUT]
        return remote(here, here, a2_send.at[i], a2_recv.at[i], device(dz=dz))

    def b2_copy(dx, dz, dy):
        i = (dx * 4 + dz) * 3 + dy - 1
        here = result.at[core, y, (z - dz) % 4, (x + dx) % 2, CUT:HEAD]
        src = here if dx or dz else own.at[CUT:HEAD]
        return remote(src, here, b2_send.at[i], b2_recv.at[i], device(dy=dy))

    def b2_arrival(dx, dz, dy):
        i = (dx * 4 + dz) * 3 + dy - 1
        here = result.at[core, (y - dy) % 4, (z - dz) % 4, (x + dx) % 2, CUT:HEAD]
        return remote(here, here, b2_send.at[i], b2_recv.at[i], device(dy=dy))

    first_steps = [(0, 2), (1, 2), (1, 0), (1, 1), (1, 3), (0, 1), (0, 3)]
    for dx, d in first_steps:
        start(a1_copy(dx, d))
        start(b1_copy(dx, d))
    for o in (2, 1, 3):
        start(a2_copy(0, 0, o))
        start(b2_copy(0, 0, o))
    arrivals = [(0, 1), (0, 3), (0, 2), (1, 0), (1, 1), (1, 3), (1, 2)]
    for dx, d in arrivals:
        a1_arrival(dx, d).wait_recv()
        for o in (2, 1, 3):
            start(a2_copy(dx, d, o))
        b1_arrival(dx, d).wait_recv()
        for o in (2, 1, 3):
            start(b2_copy(dx, d, o))
    place.wait()

    def a3_copy(whose, dx, dy):
        i = dx * 4 + dy
        here = result.at[whose, (y - dy) % 4, :, (x + dx) % 2, 0:CUT]
        return remote(here, here, c_send.at[0, i], c_recv.at[0, i], device(dc=1))

    def b3_copy(whose, dx, dz):
        i = dx * 4 + dz
        here = result.at[whose, :, (z - dz) % 4, (x + dx) % 2, CUT:HEAD]
        return remote(here, here, c_send.at[1, i], c_recv.at[1, i], device(dc=1))

    ways = [(0, 0)] + arrivals
    for dx, d in ways:
        for o in (1, 3, 2):
            a2_arrival(dx, d, o).wait_recv()
        start(a3_copy(core, dx, d))
        for o in (1, 3, 2):
            b2_arrival(dx, d, o).wait_recv()
        start(b3_copy(core, dx, d))
    for dx, d in ways:
        a3_copy(1 - core, dx, d).wait_recv()
        b3_copy(1 - core, dx, d).wait_recv()
    for copy in sent:
        copy.wait_send()


def shards(inputs, query_grads, plan):
    micro, tokens = inputs.shape[1], inputs.shape[2]
    members = lax.axis_size("dp")
    dma = pltpu.SemaphoreType.DMA
    f32, bf16 = jnp.float32, jnp.bfloat16
    vmem = pltpu.VMEM
    result = pl.pallas_call(
        functools.partial(kernel, tokens * members),
        out_shape=pltpu.VMEM((2, 4, 4, 2, HEAD, HEAD), bf16),
        in_specs=[
            pl.BlockSpec(memory_space=pl.ANY),
            pl.BlockSpec(memory_space=pl.ANY),
            pl.BlockSpec(memory_space=pltpu.SMEM),
        ],
        out_specs=pl.BlockSpec(memory_space=pl.ANY),
        scratch_shapes=[
            vmem((2, PAIRS, micro, tokens, 256), bf16),
            vmem((PAIRS, PACK, HEAD), f32),
            vmem((PAIRS, PACK, HEAD), f32),
            vmem((PAIRS, PACK, HEAD), f32),
            vmem((12, CUT, HEAD), f32),
            vmem((12, PACK - CUT, HEAD), f32),
            vmem((3, CUT, HEAD), f32),
            vmem((3, PACK - CUT, HEAD), f32),
            vmem((CUT + 8, HEAD), f32),
            vmem((4, CUT, HEAD), f32),
            vmem((4, PACK - CUT, HEAD), f32),
            vmem((PACK, HEAD), f32),
            vmem((HEAD, HEAD), bf16),
            vmem((18, 8, HEAD), f32),
            dma((2, PAIRS)),
            dma((PAIRS,)), dma((PAIRS,)),
            dma((12,)), dma((12,)), dma((12,)), dma((12,)),
            dma((3,)), dma((3,)), dma((3,)), dma((3,)),
            dma((2,)), dma((2,)),
            dma((7,)), dma((7,)), dma((7,)), dma((7,)),
            dma((24,)), dma((24,)), dma((24,)), dma((24,)),
            dma((2, 8)), dma((2, 8)),
            dma((1,)),
        ],
        compiler_params=pltpu.CompilerParams(
            collective_id=0, has_side_effects=True, vmem_limit_bytes=54 << 20
        ),
        name="factor_inverses",
    )(inputs, query_grads, plan.transpose(0, 2, 1))
    return result.reshape(1, 64, HEAD, HEAD)


def solution(mesh):
    in_specs = (
        P("section", None, "dp", None),
        P("section", None, "dp", None),
        P("section", None, None),
    )
    out_specs = P("section", None, None, None)
    return jax.shard_map(shards, mesh=mesh, in_specs=in_specs, out_specs=out_specs, check_vma=False)
```

```python
import functools

import jax
import jax.numpy as jnp
from jax import lax
from jax.experimental import pallas as pl
from jax.experimental.pallas import tpu as pltpu
from jax.sharding import PartitionSpec as P

HEAD = 128
DAMPING = 0.3
MICRO = 4
PAIRS = 16
PACK = 136
CUT = 64
MESH = pl.DeviceIdType.MESH

ORDER = (
    (2, 2), (2, 1), (1, 2),
    (2, 3), (3, 2), (1, 1),
    (1, 3), (3, 1), (3, 3),
    (2, 0), (0, 2), (1, 0), (0, 1),
    (3, 0), (0, 3), (0, 0),
)
SLOT = {offset: slot for slot, offset in enumerate(ORDER)}
GROUPS = (range(0, 3), range(3, 6), range(6, 9), range(9, 13), range(13, 16))
TURNS = tuple(
    (half, GROUPS[group])
    for half, group in ((0, 0), (0, 1), (1, 0), (0, 2), (1, 1), (0, 3), (1, 2), (0, 4), (1, 3), (1, 4))
)

def split3(x):
    high = x.astype(jnp.bfloat16)
    x = x - high.astype(jnp.float32)
    middle = x.astype(jnp.bfloat16)
    x = x - middle.astype(jnp.float32)
    return high, middle, x.astype(jnp.bfloat16)


def product(a, b):
    ah, am, al = split3(a)
    bh, bm, bl = split3(b)
    left = jnp.concatenate([ah, ah, am, ah, al, am], 0)
    right = jnp.concatenate([bh, bm, bh, bl, bh, bm], 0)
    return lax.dot_general(left, right, (((0,), (0,)), ((), ())), preferred_element_type=jnp.float32)


def spread(x):
    return jnp.broadcast_to(x, (8, HEAD))


AHEAD = 3


def invert(matrix, spot):
    lane = lax.broadcasted_iota(jnp.int32, (8, HEAD), 1)
    sub = lax.broadcasted_iota(jnp.int32, (8, HEAD), 0)
    rows = [matrix[8 * g : 8 * g + 8, :] for g in range(16)]
    for g in range(16):
        base = 8 * g
        panel = rows[g]
        inside = (lane >= base) & (lane < base + 8)
        start = jnp.where(inside, jnp.where(lane - base == sub, 1.0, 0.0), panel)
        here = (g % 2) * 9
        for j in range(8):
            spot[here + j] = spread(panel[:, base + j : base + j + 1])
        spot[here + 8] = start
        a = {(i, j): spread(spot[here + j, pl.ds(i, 1), :]) for i in range(8) for j in range(i, 8)}
        w = [spread(spot[here + 8, pl.ds(j, 1), :]) for j in range(8)]
        following = range(g + 1, min(16, g + 1 + AHEAD))
        c = {h: [spread(rows[h][:, base + j : base + j + 1]) for j in range(8)] for h in following}
        low = {}
        inverse_d = [None] * 8
        for i in (0, 2, 4, 6):
            p, q, r = a[i, i], a[i, i + 1], a[i + 1, i + 1]
            d0 = 1.0 / p
            d1 = p * (1.0 / (p * r - q * q))
            l10 = q * d0
            inverse_d[i], inverse_d[i + 1] = d0, d1
            low[i + 1, i] = l10
            e0 = {j: a[i, j] for j in range(i + 2, 8)}
            e1 = {j: a[i + 1, j] - l10 * a[i, j] for j in range(i + 2, 8)}
            for j in range(i + 2, 8):
                low[j, i], low[j, i + 1] = e0[j] * d0, e1[j] * d1
            for j in range(i + 2, 8):
                for m in range(j, 8):
                    a[j, m] = a[j, m] - (low[j, i] * e0[m] + low[j, i + 1] * e1[m])
            for v in [w, *c.values()]:
                v[i + 1] = v[i + 1] - l10 * v[i]
                for j in range(i + 2, 8):
                    v[j] = v[j] - (low[j, i] * v[i] + low[j, i + 1] * v[i + 1])
        z = [inverse_d[j] * w[j] for j in range(8)]
        ahead = {}
        for h in following:
            t = [c[h][j] * z[j] for j in range(8)]
            t = ((t[0] + t[1]) + (t[2] + t[3])) + ((t[4] + t[5]) + (t[6] + t[7]))
            ahead[h] = jnp.where(inside, 0.0, rows[h]) - t
        solved = list(z)
        for j in range(7, -1, -1):
            for i in range(j):
                solved[i] = solved[i] - low[j, i] * solved[j]

        def together(parts):
            whole = parts[7]
            for i in range(7):
                whole = jnp.where(sub == i, parts[i], whole)
            return whole

        w_rows, z_rows, solved_rows = together(w), together(z), together(solved)
        left = jnp.where(inside, 0.0, jnp.where(lane < base, -w_rows, w_rows))
        update = product(left, z_rows)
        rows = [
            solved_rows if h == g else jnp.where(inside, 0.0, rows[h]) - update[8 * h : 8 * h + 8, :]
            for h in range(16)
        ]
        for h in following:
            rows[h] = ahead[h]
    return jnp.concatenate(rows, 0)


def kernel(
    tokens_all,
    inputs_ref, grads_ref, plan_ref, result,
    data, given, taken, sums, in_y, in_z, next_z, next_y, last_in, part_z, part_y, last, own, spot,
    load_sem, core_send, core_recv, y_send, y_recv, z_send, z_recv,
    z2_send, z2_recv, y2_send, y2_recv, x_send, x_recv,
    a1_send, a1_recv, b1_send, b1_recv, a2_send, a2_recv, b2_send, b2_recv,
    c_send, c_recv, own_sem,
):
    section = lax.axis_index("section")
    dp = lax.axis_index("dp")
    z, y, x, core = dp // 16, (dp // 4) % 4, (dp // 2) % 2, dp % 2

    def device(dz=0, dy=0, dx=0, dc=0):
        there = (((z + dz) % 4) * 4 + (y + dy) % 4) * 4 + ((x + dx) % 2) * 2 + (core + dc) % 2
        return (section, there)

    def pair_of(dy, dz):
        return ((y + dy) % 4) * 4 + (z + dz) % 4

    def load(ref, half, slot):
        pair = pair_of(*ORDER[slot])
        return pltpu.make_async_copy(
            ref.at[0, :, :, pl.ds(pl.multiple_of(pair * 256, 256), 256)],
            data.at[half, slot],
            load_sem.at[half, slot],
        )

    partners = [device(dc=1)]
    partners += [device(dy=d) for d in (1, 2, 3)] + [device(dz=d) for d in (1, 2, 3)]
    partners += [device(dx=1)]
    barrier = pltpu.get_barrier_semaphore()
    for partner in partners:
        pl.semaphore_signal(barrier, inc=1, device_id=partner, device_id_type=MESH)

    for mine, refs in ((0, (grads_ref, inputs_ref)), (1, (inputs_ref, grads_ref))):

        @pl.when(core == mine)
        def _():
            for half, slots in TURNS:
                for slot in slots:
                    load(refs[half], half, slot).start()

    row = lax.broadcasted_iota(jnp.int32, (HEAD, HEAD), 0)
    col = lax.broadcasted_iota(jnp.int32, (HEAD, HEAD), 1)
    half_row = lax.broadcasted_iota(jnp.int32, (CUT, HEAD), 0)
    lane = lax.broadcasted_iota(jnp.int32, (CUT, HEAD), 1)

    def gram(half, slot):
        pair = pair_of(*ORDER[slot])
        whose = core if half else 1 - core
        factor = whose * 32 + pair * 2
        whole = data[half, slot].reshape(-1, 256)
        blocks = []
        for b in range(2):
            newest = plan_ref[0, 1, factor + b]
            own = slice(b * HEAD, (b + 1) * HEAD)
            right = [data[half, slot, 0, :, own]]
            for m in range(1, MICRO):
                kept = jnp.minimum(jnp.maximum(newest - (m - 1), 0), 1).astype(jnp.float32)
                kept = jnp.full((1, HEAD), kept, jnp.float32).astype(jnp.bfloat16)
                right.append(data[half, slot, m, :, own] * kept)
            blocks.append(
                lax.dot_general(
                    whole[:, own],
                    jnp.concatenate(right, 0),
                    (((0,), (0,)), ((), ())),
                    preferred_element_type=jnp.float32,
                )
            )
        folded = []
        for block in blocks:
            turned = pltpu.roll(block[CUT:], CUT, 1)
            folded.append(jnp.where(lane <= half_row, block[:CUT], jnp.where(lane >= CUT, block[:CUT], turned)))
        diagonals = jnp.where(lane == half_row, pltpu.roll(blocks[0][CUT:], CUT, 1), 0.0)
        diagonals += jnp.where(lane == half_row + CUT, blocks[1][CUT:], 0.0)
        return folded[0], folded[1], jnp.sum(diagonals.reshape(8, 8, HEAD), axis=0)

    def remote(src, dst, send, recv, to):
        return pltpu.make_async_remote_copy(
            src_ref=src, dst_ref=dst, send_sem=send, recv_sem=recv, device_id=to, device_id_type=MESH
        )

    sent = []

    def start(copy):
        copy.start()
        sent.append(copy)

    def core_copy(slot):
        return remote(given.at[slot], taken.at[slot], core_send.at[slot], core_recv.at[slot], device(dc=1))

    def y_copy(dy, dz):
        slot = SLOT[dy, dz]
        i = (dy - 1) * 4 + dz
        return remote(sums.at[slot, 0:CUT], in_y.at[i], y_send.at[i], y_recv.at[i], device(dy=dy))

    def z_copy(dy, dz):
        slot = SLOT[dy, dz]
        i = (dz - 1) * 4 + dy
        return remote(sums.at[slot, CUT:PACK], in_z.at[i], z_send.at[i], z_recv.at[i], device(dz=dz))

    def work_other(slots):
        for slot in slots:
            load(inputs_ref, 0, slot).wait()
        for slot in slots:
            one, two, diagonals = gram(0, slot)
            given[slot, 0:CUT] = one
            given[slot, CUT:HEAD] = two
            given[slot, HEAD:PACK] = diagonals
        if slots[0] == 0:
            pl.semaphore_wait(barrier, len(partners))
        for slot in slots:
            start(core_copy(slot))

    def work_own(slots):
        for slot in slots:
            load(inputs_ref, 1, slot).wait()
        for slot in slots:
            one, two, diagonals = gram(1, slot)
            sums[slot, 0:CUT] = one
            sums[slot, CUT:HEAD] = two
            sums[slot, HEAD:PACK] = diagonals
        for slot in slots:
            core_copy(slot).wait_recv()
            sums[slot] += taken[slot]
            dy, dz = ORDER[slot]
            if dy:
                start(y_copy(dy, dz))
            if dz:
                start(z_copy(dy, dz))

    for half, slots in TURNS:
        (work_own if half else work_other)(slots)

    def z2_copy(dz):
        return remote(part_z.at[dz], next_z.at[dz - 1], z2_send.at[dz - 1], z2_recv.at[dz - 1], device(dz=dz))

    def y2_copy(dy):
        return remote(part_y.at[dy], next_y.at[dy - 1], y2_send.at[dy - 1], y2_recv.at[dy - 1], device(dy=dy))

    for d in (2, 1, 3, 0):
        for o in (1, 2, 3):
            y_copy(o, d).wait_recv()
        part_z[d] = (sums[SLOT[0, d], 0:CUT] + in_y[d]) + (in_y[4 + d] + in_y[8 + d])
        if d:
            start(z2_copy(d))
        for o in (1, 2, 3):
            z_copy(d, o).wait_recv()
        part_y[d] = (sums[SLOT[d, 0], CUT:PACK] + in_z[d]) + (in_z[4 + d] + in_z[8 + d])
        if d:
            start(y2_copy(d))

    def rows_of(which):
        return pl.ds(pl.multiple_of(which * CUT, CUT), CUT)

    def x_copy(part):
        src, dst = ((rows_of(1 - x), slice(0, CUT)), (slice(HEAD, PACK), slice(CUT, CUT + 8)))[part]
        return remote(last.at[src], last_in.at[dst], x_send.at[part], x_recv.at[part], device(dx=1))

    for d in (1, 3, 2):
        z2_copy(d).wait_recv()
        y2_copy(d).wait_recv()
    last[0:CUT] = (part_z[0] + next_z[0]) + (next_z[1] + next_z[2])
    last[CUT:PACK] = (part_y[0] + next_y[0]) + (next_y[1] + next_y[2])
    start(x_copy(0))
    start(x_copy(1))
    x_copy(0).wait_recv()
    x_copy(1).wait_recv()

    folded = last[rows_of(x)] + last_in[0:CUT]
    diagonals = jnp.sum(last[HEAD:PACK] + last_in[CUT : CUT + 8], axis=0, keepdims=True)
    second = x.astype(jnp.float32)
    diagonals = second * diagonals + (1.0 - second) * pltpu.roll(jnp.broadcast_to(diagonals, (8, HEAD)), CUT, 1)[0:1]
    unfolded = jnp.concatenate([folded, pltpu.roll(folded, CUT, 1)], 0)
    stored = ((row < CUT) & ((col >= CUT) | (col < row))) | ((row >= CUT) & (col > row))
    triangle = jnp.where(stored, unfolded, 0.0)
    total = triangle + triangle.T + jnp.where(row == col, jnp.where(row < CUT, unfolded, diagonals), 0.0)
    newest = plan_ref[0, 1, core * 32 + pair_of(0, 0) * 2 + x]
    count = jnp.full((1, HEAD), (newest + 1).astype(jnp.float32), jnp.float32) * float(tokens_all)
    damped = total / count + jnp.where(row == col, DAMPING, 0.0)
    inverse = invert(damped, spot)
    own[...] = inverse.astype(jnp.bfloat16)
    place = pltpu.make_async_copy(own, result.at[core, y, z, x], own_sem.at[0])
    place.start()

    def a1_copy(dx, dy):
        i = dx * 4 + dy - 1
        here = result.at[core, y, z, x, 0:CUT]
        return remote(own.at[0:CUT], here, a1_send.at[i], a1_recv.at[i], device(dx=dx, dy=dy))

    def b1_copy(dx, dz):
        i = dx * 4 + dz - 1
        here = result.at[core, y, z, x, CUT:HEAD]
        return remote(own.at[CUT:HEAD], here, b1_send.at[i], b1_recv.at[i], device(dx=dx, dz=dz))

    def a1_arrival(dx, dy):
        i = dx * 4 + dy - 1
        here = result.at[core, (y - dy) % 4, z, (x + dx) % 2, 0:CUT]
        return remote(here, here, a1_send.at[i], a1_recv.at[i], device(dx=dx, dy=dy))

    def b1_arrival(dx, dz):
        i = dx * 4 + dz - 1
        here = result.at[core, y, (z - dz) % 4, (x + dx) % 2, CUT:HEAD]
        return remote(here, here, b1_send.at[i], b1_recv.at[i], device(dx=dx, dz=dz))

    def a2_copy(dx, dy, dz):
        i = (dx * 4 + dy) * 3 + dz - 1
        here = result.at[core, (y - dy) % 4, z, (x + dx) % 2, 0:CUT]
        src = here if dx or dy else own.at[0:CUT]
        return remote(src, here, a2_send.at[i], a2_recv.at[i], device(dz=dz))

    def a2_arrival(dx, dy, dz):
        i = (dx * 4 + dy) * 3 + dz - 1
        here = result.at[core, (y - dy) % 4, (z - dz) % 4, (x + dx) % 2, 0:CUT]
        return remote(here, here, a2_send.at[i], a2_recv.at[i], device(dz=dz))

    def b2_copy(dx, dz, dy):
        i = (dx * 4 + dz) * 3 + dy - 1
        here = result.at[core, y, (z - dz) % 4, (x + dx) % 2, CUT:HEAD]
        src = here if dx or dz else own.at[CUT:HEAD]
        return remote(src, here, b2_send.at[i], b2_recv.at[i], device(dy=dy))

    def b2_arrival(dx, dz, dy):
        i = (dx * 4 + dz) * 3 + dy - 1
        here = result.at[core, (y - dy) % 4, (z - dz) % 4, (x + dx) % 2, CUT:HEAD]
        return remote(here, here, b2_send.at[i], b2_recv.at[i], device(dy=dy))

    first_steps = [(0, 2), (1, 2), (1, 0), (1, 1), (1, 3), (0, 1), (0, 3)]
    for dx, d in first_steps:
        start(a1_copy(dx, d))
        start(b1_copy(dx, d))
    for o in (2, 1, 3):
        start(a2_copy(0, 0, o))
        start(b2_copy(0, 0, o))
    arrivals = [(0, 1), (0, 3), (0, 2), (1, 0), (1, 1), (1, 3), (1, 2)]
    for dx, d in arrivals:
        a1_arrival(dx, d).wait_recv()
        for o in (2, 1, 3):
            start(a2_copy(dx, d, o))
        b1_arrival(dx, d).wait_recv()
        for o in (2, 1, 3):
            start(b2_copy(dx, d, o))
    place.wait()

    def a3_copy(whose, dx, dy):
        i = dx * 4 + dy
        here = result.at[whose, (y - dy) % 4, :, (x + dx) % 2, 0:CUT]
        return remote(here, here, c_send.at[0, i], c_recv.at[0, i], device(dc=1))

    def b3_copy(whose, dx, dz):
        i = dx * 4 + dz
        here = result.at[whose, :, (z - dz) % 4, (x + dx) % 2, CUT:HEAD]
        return remote(here, here, c_send.at[1, i], c_recv.at[1, i], device(dc=1))

    ways = [(0, 0)] + arrivals
    for dx, d in ways:
        for o in (1, 3, 2):
            a2_arrival(dx, d, o).wait_recv()
        start(a3_copy(core, dx, d))
        for o in (1, 3, 2):
            b2_arrival(dx, d, o).wait_recv()
        start(b3_copy(core, dx, d))
    for dx, d in ways:
        a3_copy(1 - core, dx, d).wait_recv()
        b3_copy(1 - core, dx, d).wait_recv()
    for copy in sent:
        copy.wait_send()


def shards(inputs, query_grads, plan):
    micro, tokens = inputs.shape[1], inputs.shape[2]
    members = lax.axis_size("dp")
    dma = pltpu.SemaphoreType.DMA
    f32, bf16 = jnp.float32, jnp.bfloat16
    vmem = pltpu.VMEM
    result = pl.pallas_call(
        functools.partial(kernel, tokens * members),
        out_shape=pltpu.VMEM((2, 4, 4, 2, HEAD, HEAD), bf16),
        in_specs=[
            pl.BlockSpec(memory_space=pl.ANY),
            pl.BlockSpec(memory_space=pl.ANY),
            pl.BlockSpec(memory_space=pltpu.SMEM),
        ],
        out_specs=pl.BlockSpec(memory_space=pl.ANY),
        scratch_shapes=[
            vmem((2, PAIRS, micro, tokens, 256), bf16),
            vmem((PAIRS, PACK, HEAD), f32),
            vmem((PAIRS, PACK, HEAD), f32),
            vmem((PAIRS, PACK, HEAD), f32),
            vmem((12, CUT, HEAD), f32),
            vmem((12, PACK - CUT, HEAD), f32),
            vmem((3, CUT, HEAD), f32),
            vmem((3, PACK - CUT, HEAD), f32),
            vmem((CUT + 8, HEAD), f32),
            vmem((4, CUT, HEAD), f32),
            vmem((4, PACK - CUT, HEAD), f32),
            vmem((PACK, HEAD), f32),
            vmem((HEAD, HEAD), bf16),
            vmem((18, 8, HEAD), f32),
            dma((2, PAIRS)),
            dma((PAIRS,)), dma((PAIRS,)),
            dma((12,)), dma((12,)), dma((12,)), dma((12,)),
            dma((3,)), dma((3,)), dma((3,)), dma((3,)),
            dma((2,)), dma((2,)),
            dma((7,)), dma((7,)), dma((7,)), dma((7,)),
            dma((24,)), dma((24,)), dma((24,)), dma((24,)),
            dma((2, 8)), dma((2, 8)),
            dma((1,)),
        ],
        compiler_params=pltpu.CompilerParams(
            collective_id=0, has_side_effects=True, vmem_limit_bytes=54 << 20
        ),
        name="factor_inverses",
    )(inputs, query_grads, plan.transpose(0, 2, 1))
    return result.reshape(1, 64, HEAD, HEAD)


def solution(mesh):
    in_specs = (
        P("section", None, "dp", None),
        P("section", None, "dp", None),
        P("section", None, None),
    )
    out_specs = P("section", None, None, None)
    return jax.shard_map(shards, mesh=mesh, in_specs=in_specs, out_specs=out_specs, check_vma=False)
```
